32 devices in a mesh: space: 8 (over z, x), group: 4 (over y, core).
Axes of the slice: x: 2, y: 2, z: 4, core: 2. Of those that a mesh axis runs over, the one named last changes fastest.
Arguments:
- point_feats: bfloat16 [32768, 32], P(('space', 'group')), may hold values from -6 to 6
- point_voxel: int32 [32768], P(('space', 'group')), may hold values from -1 to 4095, as said below
- cotangent: bfloat16 [32768, 32], P(('space', 'group')), may hold values from -6 to 6
- kernel: bfloat16 [3, 3, 3, 32, 32], replicated, may hold values from -0.21875 to 0.21875
Outputs:
- point_grad: bfloat16 [32768, 32], P(('space', 'group'))
The draws below stay inside these ranges and needn't reach their ends.
Inputs may be any that keep to these rules, and one draw needn't show every extreme that they name: `point_voxel`: in each block of 256 slots that one device sends to one member of its group the live slots come first and hold voxel numbers below 4096, the rest -1; every device fills one of its blocks completely.
All inputs are finite; a program needn't handle non-finite values.
Results may differ from the reference program's by a relative error of at most 0.0049.
Values may be sent and summed in bfloat16 or wider, within the bound.
A program may use at most 64 MiB of HBM per device.

```python
import jax
import jax.numpy as jnp
from jax import lax

C = 32
XD = 16
YD = 16
ZB = 16
CAP = 256
V_DEV = 4096
NX = 128
NY = 64
NPTS = 32768
N_GROUP = 4


def draw_point_voxel(key, part):
    key_live, key_full, key_vox = jax.random.split(key, 3)
    blocks = NPTS // CAP
    live = jax.random.randint(key_live, (blocks,), 1, CAP + 1)
    senders = blocks // N_GROUP
    full = jax.random.randint(key_full, (senders,), 0, N_GROUP)
    number = jnp.arange(blocks)
    live = jnp.where(number % N_GROUP == full[number // N_GROUP], CAP, live)
    voxels = jax.random.randint(key_vox, (blocks, CAP), 0, V_DEV)
    slot = jnp.arange(CAP)[None, :]
    return jnp.where(slot < live[:, None], voxels, -1).reshape(NPTS).astype(jnp.int32)


def shard_levels(key, dims, shards, smallest, largest):
    def one(position, shards_of):
        heights = jax.random.uniform(jax.random.fold_in(jax.random.fold_in(key, 6), position), (shards_of,), jnp.float32, smallest / len(shards), largest / len(shards))
        return jnp.repeat(jnp.exp(heights), dims[position] // shards_of).reshape((-1,) + (1,) * (len(dims) - position - 1))

    factor_of = one(*shards[0])
    for cut in shards[1:]:
        factor_of = factor_of * one(*cut)
    return factor_of


def gaussian(key, shape, spread, bound, cuts=(), held_as=jnp.bfloat16):
    factor_of = shard_levels(key, shape, cuts, -0.22, 0.18) if cuts else 1.0
    result = jax.random.normal(key, shape, jnp.float32) * spread * factor_of
    return jnp.minimum(jnp.maximum(result, -bound), bound).astype(held_as)


def setup_inputs(seed: int = 0) -> dict:
    splits = jax.random.split(jax.random.key(seed), 5)
    point_feats = gaussian(splits[0], (NPTS, C), 1.0, 6.0, ((0, 32),))
    point_voxel = draw_point_voxel(jax.random.fold_in(splits[4], 71), 0)
    cotangent = gaussian(splits[2], (NPTS, C), 1.0, 6.0, ((0, 32),))
    kernel = gaussian(splits[3], (3, 3, 3, C, C), (27 * C) ** -0.5, 0.21875)
    return {"point_feats": point_feats, "point_voxel": point_voxel, "cotangent": cotangent, "kernel": kernel}


def convolve(padded, weights):
    return lax.conv_general_dilated(padded[None], weights, (1, 1, 1), "VALID", dimension_numbers=("NDHWC", "DHWIO", "NDHWC"), preferred_element_type=jnp.float32)[0]


def reference(point_feats, point_voxel, cotangent, kernel):
    rows = point_voxel.shape[0]
    order = jnp.arange(rows, dtype=jnp.int32)
    device = order // (N_GROUP * CAP)
    sx = device // N_GROUP
    block = (order % (N_GROUP * CAP)) // CAP
    live = point_voxel >= 0
    safe = jnp.where(live, point_voxel, 0)
    xl = safe // (YD * ZB)
    yl = (safe // ZB) % YD
    zl = safe % ZB
    total = NX * NY * ZB
    flat = ((sx * XD + xl) * NY + block * YD + yl) * ZB + zl
    flat = jnp.where(live, flat, total).astype(jnp.int32)
    sums = jax.ops.segment_sum(point_feats.astype(jnp.float32), flat, total + 1)
    counts = jax.ops.segment_sum(jnp.ones((rows,), jnp.float32), flat, total + 1)
    divisor = jnp.maximum(counts, 1.0)
    mean = (sums / divisor[:, None])[:total].reshape(NX, NY, ZB, C).astype(jnp.bfloat16)
    out = convolve(jnp.pad(mean, ((1, 1), (1, 1), (1, 1), (0, 0))), kernel)
    gy = jax.ops.segment_sum(cotangent.astype(jnp.float32), flat, total + 1)[:total].reshape(NX, NY, ZB, C)
    sig = jax.nn.sigmoid(out)
    gout = (gy * sig * (1.0 + out * (1.0 - sig))).astype(jnp.bfloat16)
    flipped = jnp.swapaxes(kernel[::-1, ::-1, ::-1], 3, 4)
    ggrid = convolve(jnp.pad(gout, ((1, 1), (1, 1), (1, 1), (0, 0))), flipped)
    table = jnp.concatenate([ggrid.reshape(total, C), jnp.zeros((1, C), jnp.float32)], axis=0)
    return (table[flat] / divisor[flat][:, None]).astype(jnp.bfloat16)
```

```python
import functools

import jax
import jax.numpy as jnp
from jax import lax
from jax.experimental import pallas as pl
from jax.experimental.pallas import tpu as pltpu
from jax.sharding import PartitionSpec as P

MESH = pl.DeviceIdType.MESH
F32 = jnp.float32
BF16 = jnp.bfloat16
SIDE = 16
C = 32
COLS = SIDE * SIDE
LANES = SIDE * C
HALF = LANES // 2
CAP = 256

WAYS = ((-1, 0), (1, 0), (0, -1), (0, 1), (-1, -1), (-1, 1), (1, -1), (1, 1))


def nt(a, b):
    return lax.dot_general(a, b, (((1,), (1,)), ((), ())), preferred_element_type=F32)


def nn(a, b):
    return jnp.dot(a, b, preferred_element_type=F32)


def kernel(
    n, ns, feats, cots, vox, weights, out,
    gotf, gotc, gotv, hot, masked, tiled, bmf, bef, bmb, beb,
    inner, hx, hy, xm, xe, xh, acc, gy, div, back,
    fs, fr, cs, cr, vs, vr, hs, hr, rs, rr,
):
    s = lax.axis_index("space")
    g = lax.axis_index("group")

    def exists(way):
        ok = None
        for d, at, size in ((way[0], s, ns), (way[1], g, n)):
            if d == 0:
                continue
            here = at > 0 if d < 0 else at < size - 1
            ok = here if ok is None else jnp.logical_and(ok, here)
        return ok

    def peer(d):
        return lax.rem(g + d, n)

    barrier = pltpu.get_barrier_semaphore()
    outer = [w for w in WAYS if w[0] != 0]
    for d in range(1, n):
        pl.semaphore_signal(barrier, inc=1, device_id=(s, peer(d)), device_id_type=MESH)
    for w in outer:
        @pl.when(exists(w))
        def _(w=w):
            pl.semaphore_signal(barrier, inc=1, device_id=(s + w[0], g + w[1]), device_id_type=MESH)

    peers = n - 1
    for w in outer:
        peers = peers + jnp.where(exists(w), 1, 0)
    pl.semaphore_wait(barrier, peers)

    def slots_of(k):
        return pl.ds(pl.multiple_of(k * CAP, CAP), CAP)

    def copy_v(d):
        return pltpu.make_async_remote_copy(
            src_ref=vox.at[peer(d)], dst_ref=gotv.at[d], send_sem=vs.at[d], recv_sem=vr.at[d],
            device_id=(s, peer(d)), device_id_type=MESH)

    def copy_f(d):
        return pltpu.make_async_remote_copy(
            src_ref=feats.at[:, slots_of(peer(d))], dst_ref=gotf.at[d], send_sem=fs.at[d], recv_sem=fr.at[d],
            device_id=(s, peer(d)), device_id_type=MESH)

    def copy_c(d):
        return pltpu.make_async_remote_copy(
            src_ref=cots.at[:, slots_of(peer(d))], dst_ref=gotc.at[d], send_sem=cs.at[d], recv_sem=cr.at[d],
            device_id=(s, peer(d)), device_id_type=MESH)

    for d in range(1, n):
        copy_v(d).start()
        copy_f(d).start()
        copy_c(d).start()

    spread = jnp.where(
        (lax.broadcasted_iota(jnp.int32, (C, HALF), 1) & (C - 1)) == lax.broadcasted_iota(jnp.int32, (C, HALF), 0),
        1.0, 0.0).astype(BF16)
    tiled[...] = nn(weights[...], spread)
    block = lax.broadcasted_iota(jnp.int32, (C, HALF), 1) // C
    narrow = lax.broadcasted_iota(jnp.int32, (C, 128), 1) // C
    none = jnp.zeros((C, 128), BF16)
    wide = HALF // C

    def tile(dx, dy, dz):
        a = (dx * 3 + dy) * 3 + dz
        return tiled[a * C : (a + 1) * C, :]

    for dy in range(3):
        for dz in range(3):
            w0, w1, w2 = (tile(dx, dy, dz) for dx in range(3))
            fy, fz = 2 - dy, 2 - dz
            for i in range(wide):
                band = jnp.where(
                    block == i, w1, jnp.where(block == i - 1, w2, jnp.where(block == i + 1, w0, 0.0))
                ).astype(BF16)
                bmf[dy, dz * HALF + i * C : dz * HALF + (i + 1) * C, :] = band
                bmb[fy, i * C : (i + 1) * C, fz * HALF : (fz + 1) * HALF] = band
                if i == wide - 1:
                    edge = jnp.where(narrow == 0, w0[:, :128], 0.0).astype(BF16)
                elif i == 0:
                    edge = jnp.where(narrow == 3, w2[:, :128], 0.0).astype(BF16)
                else:
                    edge = none
                beb[fy, i * C : (i + 1) * C, fz * 128 : (fz + 1) * 128] = edge
            bef[dy, dz * 128 : dz * 128 + C, :] = jnp.where(block == wide - 1, w2, 0.0).astype(BF16)
            bef[dy, dz * 128 + C : dz * 128 + 3 * C, :] = jnp.zeros((2 * C, HALF), BF16)
            bef[dy, dz * 128 + 3 * C : dz * 128 + 4 * C, :] = jnp.where(block == 0, w0, 0.0).astype(BF16)

    for p in range(2):
        for side, d in ((0, -1), (1, 1)):
            @pl.when(jnp.logical_not(exists((d, 0))))
            def _(p=p, side=side):
                hx[p, side] = jnp.zeros((COLS + 2 * SIDE, 128), BF16)

            @pl.when(jnp.logical_not(exists((0, d))))
            def _(p=p, side=side):
                hy[p, side] = jnp.zeros((SIDE, LANES), BF16)
                r0 = side * (COLS + SIDE)
                for q in range(2):
                    hx[p, q, r0 : r0 + SIDE, :] = jnp.zeros((SIDE, 128), BF16)
    for b in range(2):
        xm[b, 0:SIDE, :] = jnp.zeros((SIDE, 3 * HALF), BF16)
        xm[b, COLS + SIDE : COLS + 2 * SIDE, :] = jnp.zeros((SIDE, 3 * HALF), BF16)

    row = lax.broadcasted_iota(jnp.int32, (COLS, CAP), 0)

    def place(d, v, f, c):
        lo = v & (COLS - 1)
        hi = v >> 8
        at = slice(d * CAP, (d + 1) * CAP)
        hot[:, at] = jnp.where(row == lo, 1.0, 0.0).astype(BF16)
        f = f.astype(F32)
        c = c.astype(F32)
        hi = jnp.broadcast_to(hi, (C, CAP))
        for x in range(SIDE):
            hit = hi == x
            for q, val in enumerate((f, c, 1.0)):
                r0 = q * LANES + x * C
                masked[r0 : r0 + C, at] = jnp.where(hit, val, 0.0).astype(BF16)

    place(0, vox[g], feats[:, slots_of(g)], cots[:, slots_of(g)])
    for d in range(1, n):
        copy_v(d).wait_recv()
        copy_f(d).wait_recv()
        copy_c(d).wait_recv()
        place(d, gotv[d], gotf[d], gotc[d])

    pooled = nt(hot[...], masked[...])
    count = jnp.maximum(pooled[:, 2 * LANES :], 1.0)
    div[...] = count
    gy[...] = pooled[:, LANES : 2 * LANES]
    mean = (pooled[:, :LANES] / count).astype(BF16)

    def shifts(val):
        z = lax.broadcasted_iota(jnp.int32, val.shape, 0) & (SIDE - 1)
        down = jnp.where(z == 0, 0.0, pltpu.roll(val, 1, 0))
        up = jnp.where(z == SIDE - 1, 0.0, pltpu.roll(val, val.shape[0] - 1, 0))
        return down.astype(BF16), val.astype(BF16), up.astype(BF16)

    def halo(p, k):
        dx, dy = WAYS[k]
        src_rows = pl.ds(0, SIDE) if dy < 0 else pl.ds(COLS - SIDE, SIDE) if dy > 0 else pl.ds(0, COLS)
        if dx == 0:
            src = inner.at[p, src_rows, :]
            dst = hy.at[p, 0 if dy > 0 else 1]
        else:
            src = inner.at[p, src_rows, pl.ds(0 if dx < 0 else LANES - 128, 128)]
            dst_rows = pl.ds(0, SIDE) if dy > 0 else pl.ds(COLS + SIDE, SIDE) if dy < 0 else pl.ds(SIDE, COLS)
            dst = hx.at[p, 0 if dx > 0 else 1, dst_rows, :]
        return pltpu.make_async_remote_copy(
            src_ref=src, dst_ref=dst, send_sem=hs.at[p, k], recv_sem=hr.at[p, k],
            device_id=(s + dx, g + dy), device_id_type=MESH)

    def convolve(p, val, main, edges, dot):
        inner[p] = val
        for k, w in enumerate(WAYS):
            @pl.when(exists(w))
            def _(k=k):
                halo(p, k).start()
        for b in range(2):
            for j, part in enumerate(shifts(val[:, b * HALF : (b + 1) * HALF].astype(F32))):
                xm[b, SIDE : SIDE + COLS, j * HALF : (j + 1) * HALF] = part
        total = None
        for dy in range(3):
            lhs = xm[:, dy * SIDE : dy * SIDE + COLS, :].reshape(2 * COLS, 3 * HALF)
            term = dot(lhs, main[dy])
            total = term if total is None else total + term
        acc[...] = total.reshape(2, COLS, HALF)
        for k, w in enumerate(WAYS):
            @pl.when(exists((-w[0], -w[1])))
            def _(k=k):
                halo(p, k).wait_recv()
        for side in range(2):
            rim = hy[p, side].astype(F32)
            for b in range(2):
                for j, part in enumerate(shifts(rim[:, b * HALF : (b + 1) * HALF])):
                    xh[side, b, :, j * HALF : (j + 1) * HALF] = part
        span = COLS + 2 * SIDE
        first = lax.broadcasted_iota(jnp.int32, (span, 128), 1) < C
        for b in range(2):
            at = slice(HALF, HALF + 128) if b == 0 else slice(HALF - 128, HALF)
            own = jnp.concatenate([hy[p, 0, :, at], inner[p, :, at], hy[p, 1, :, at]], axis=0).astype(F32)
            far = hx[p, b].astype(F32)
            edge = jnp.where(first, own, far) if b == 0 else jnp.where(first, far, own)
            for j, part in enumerate(shifts(edge)):
                xe[b, :, j * 128 : (j + 1) * 128] = part
        total = None
        for dy in range(3):
            lhs = xe[:, dy * SIDE : dy * SIDE + COLS, :].reshape(2 * COLS, 3 * 128)
            term = dot(lhs, edges[dy])
            total = term if total is None else total + term
        acc[...] += total.reshape(2, COLS, HALF)
        for side, dy, r0 in ((0, 0, 0), (1, 2, COLS - SIDE)):
            term = dot(xh[side].reshape(2 * SIDE, 3 * HALF), main[dy])
            acc[:, r0 : r0 + SIDE, :] += term.reshape(2, SIDE, HALF)

    convolve(0, mean, bmf, bef, nn)
    parts = []
    for b in range(2):
        o = acc[b]
        sig = 1.0 / (1.0 + jnp.exp(-o))
        parts.append((gy[:, b * HALF : (b + 1) * HALF] * sig * (1.0 + o * (1.0 - sig))).astype(BF16))
    convolve(1, jnp.concatenate(parts, axis=1), bmb, beb, nt)

    grad = jnp.concatenate([acc[b] / div[:, b * HALF : (b + 1) * HALF] for b in range(2)], axis=1)
    grad = jnp.transpose(grad).astype(BF16)

    def copy_r(d):
        return pltpu.make_async_remote_copy(
            src_ref=back.at[d], dst_ref=out.at[:, slots_of(g)], send_sem=rs.at[d], recv_sem=rr.at[d],
            device_id=(s, peer(n - d)), device_id_type=MESH)

    for d in list(range(1, n)) + [0]:
        v = vox[g] if d == 0 else gotv[d]
        hi = jnp.broadcast_to(v >> 8, (C, CAP))
        rows = nn(grad, hot[:, d * CAP : (d + 1) * CAP])
        picked = jnp.zeros((C, CAP), F32)
        for x in range(SIDE):
            picked = picked + jnp.where(hi == x, rows[x * C : (x + 1) * C], 0.0)
        if d == 0:
            out[:, slots_of(g)] = picked.astype(BF16)
        else:
            back[d] = picked.astype(BF16)
            copy_r(d).start()
    for d in range(1, n):
        copy_r(d).wait_recv()
    for d in range(1, n):
        copy_v(d).wait_send()
        copy_f(d).wait_send()
        copy_c(d).wait_send()
        copy_r(d).wait_send()
    for p in range(2):
        for k, w in enumerate(WAYS):
            @pl.when(exists(w))
            def _(p=p, k=k):
                halo(p, k).wait_send()


def per_device(n, ns, point_feats, point_voxel, cotangent, weights):
    slots = n * CAP
    span = COLS + 2 * SIDE
    vm = pltpu.VMEM
    dma = pltpu.SemaphoreType.DMA
    return pl.pallas_call(
        functools.partial(kernel, n, ns),
        out_shape=jax.ShapeDtypeStruct((C, slots), BF16),
        in_specs=[pl.BlockSpec(memory_space=vm)] * 4,
        out_specs=pl.BlockSpec(memory_space=vm),
        scratch_shapes=[
            vm((n, C, CAP), BF16),
            vm((n, C, CAP), BF16),
            vm((n, 1, CAP), jnp.int32),
            vm((COLS, slots), BF16),
            vm((3 * LANES, slots), BF16),
            vm((27 * C, HALF), F32),
            vm((3, 3 * HALF, HALF), BF16),
            vm((3, 3 * 128, HALF), BF16),
            vm((3, HALF, 3 * HALF), BF16),
            vm((3, HALF, 3 * 128), BF16),
            vm((2, COLS, LANES), BF16),
            vm((2, 2, span, 128), BF16),
            vm((2, 2, SIDE, LANES), BF16),
            vm((2, span, 3 * HALF), BF16),
            vm((2, span, 3 * 128), BF16),
            vm((2, 2, SIDE, 3 * HALF), BF16),
            vm((2, COLS, HALF), F32),
            vm((COLS, LANES), F32),
            vm((COLS, LANES), F32),
            vm((n, C, CAP), BF16),
            dma((n,)), dma((n,)), dma((n,)), dma((n,)), dma((n,)), dma((n,)),
            dma((2, 8)), dma((2, 8)), dma((n,)), dma((n,)),
        ],
        compiler_params=pltpu.CompilerParams(
            collective_id=0, has_side_effects=True, vmem_limit_bytes=48 * 2**20
        ),
    )(point_feats.T, cotangent.T, point_voxel.reshape(n, 1, CAP), weights.reshape(27 * C, C)).T


def solution(mesh):
    n, ns = mesh.shape["group"], mesh.shape["space"]
    placed = (P(("space", "group"), None), P(("space", "group")), P(("space", "group"), None), P())
    return jax.shard_map(
        functools.partial(per_device, n, ns),
        mesh=mesh,
        in_specs=placed,
        out_specs=P(("space", "group"), None),
        check_vma=False,
    )
```

```python
import functools

import jax
import jax.numpy as jnp
from jax import lax
from jax.experimental import pallas as pl
from jax.experimental.pallas import tpu as pltpu
from jax.sharding import PartitionSpec as P

MESH = pl.DeviceIdType.MESH
F32 = jnp.float32
BF16 = jnp.bfloat16
SIDE = 16
C = 32
COLS = SIDE * SIDE
LANES = SIDE * C
HALF = LANES // 2
CAP = 256

WAYS = ((-1, 0), (1, 0), (0, -1), (0, 1), (-1, -1), (-1, 1), (1, -1), (1, 1))


def nt(a, b):
    return lax.dot_general(a, b, (((1,), (1,)), ((), ())), preferred_element_type=F32)


def nn(a, b):
    return jnp.dot(a, b, preferred_element_type=F32)


def kernel(
    n, ns, feats, cots, vox, weights, out,
    gotf, gotc, gotv, w_in, hot, masked, sums, tiled, bmf, bef, bmb, beb,
    inner, packed, hx, hc, hy, xm, xe, xh, acc, gy, div, back,
    local, fs, fr, cs, cr, vs, vr, hs, hr, rs, rr,
):
    s = lax.axis_index("space")
    g = lax.axis_index("group")

    def exists(way):
        ok = None
        for d, at, size in ((way[0], s, ns), (way[1], g, n)):
            if d == 0:
                continue
            here = at > 0 if d < 0 else at < size - 1
            ok = here if ok is None else jnp.logical_and(ok, here)
        return ok

    def peer(d):
        return lax.rem(g + d, n)

    def slots_of(k):
        return pl.ds(pl.multiple_of(k * CAP, CAP), CAP)

    own_copies = [
        pltpu.make_async_copy(src, dst, local.at[i])
        for i, (src, dst) in enumerate((
            (weights, w_in), (vox.at[g], gotv.at[0]),
            (feats.at[:, slots_of(g)], gotf.at[0]), (cots.at[:, slots_of(g)], gotc.at[0])))
    ]
    for c in own_copies:
        c.start()

    barrier = pltpu.get_barrier_semaphore()
    outer = [w for w in WAYS if w[0] != 0]
    for d in range(1, n):
        pl.semaphore_signal(barrier, inc=1, device_id=(s, peer(d)), device_id_type=MESH)
    for w in outer:
        @pl.when(exists(w))
        def _(w=w):
            pl.semaphore_signal(barrier, inc=1, device_id=(s + w[0], g + w[1]), device_id_type=MESH)

    peers = n - 1
    for w in outer:
        peers = peers + jnp.where(exists(w), 1, 0)
    pl.semaphore_wait(barrier, peers)

    def copy_v(d):
        return pltpu.make_async_remote_copy(
            src_ref=vox.at[peer(d)], dst_ref=gotv.at[d], send_sem=vs.at[d], recv_sem=vr.at[d],
            device_id=(s, peer(d)), device_id_type=MESH)

    def copy_f(d):
        return pltpu.make_async_remote_copy(
            src_ref=feats.at[:, slots_of(peer(d))], dst_ref=gotf.at[d], send_sem=fs.at[d], recv_sem=fr.at[d],
            device_id=(s, peer(d)), device_id_type=MESH)

    def copy_c(d):
        return pltpu.make_async_remote_copy(
            src_ref=cots.at[:, slots_of(peer(d))], dst_ref=gotc.at[d], send_sem=cs.at[d], recv_sem=cr.at[d],
            device_id=(s, peer(d)), device_id_type=MESH)

    for d in range(1, n):
        copy_v(d).start()
        copy_f(d).start()
    for d in range(1, n):
        copy_c(d).start()
    for c in own_copies:
        c.wait()

    spread = jnp.where(
        (lax.broadcasted_iota(jnp.int32, (C, HALF), 1) & (C - 1)) == lax.broadcasted_iota(jnp.int32, (C, HALF), 0),
        1.0, 0.0).astype(BF16)
    tiled[...] = nn(w_in[...], spread)
    block = lax.broadcasted_iota(jnp.int32, (C, HALF), 1) // C
    narrow = lax.broadcasted_iota(jnp.int32, (C, 128), 1) // C
    none = jnp.zeros((C, 128), BF16)
    wide = HALF // C

    def tile(dx, dy, dz):
        a = (dx * 3 + dy) * 3 + dz
        return tiled[a * C : (a + 1) * C, :]

    def band(i, w0, w1, w2):
        inside = jnp.where(block == i, w1, jnp.where(block == i - 1, w2, jnp.where(block == i + 1, w0, 0.0)))
        return inside.astype(BF16)

    def forward_bands():
        for dy in range(3):
            for dz in range(3):
                w0, w1, w2 = (tile(dx, dy, dz) for dx in range(3))
                for i in range(wide):
                    bmf[dy, dz * HALF + i * C : dz * HALF + (i + 1) * C, :] = band(i, w0, w1, w2)
                bef[dy, dz * 128 : dz * 128 + C, :] = jnp.where(block == wide - 1, w2, 0.0).astype(BF16)
                bef[dy, dz * 128 + C : dz * 128 + 3 * C, :] = jnp.zeros((2 * C, HALF), BF16)
                bef[dy, dz * 128 + 3 * C : dz * 128 + 4 * C, :] = jnp.where(block == 0, w0, 0.0).astype(BF16)

    def backward_bands():
        for fy in range(3):
            for fz in range(3):
                w0, w1, w2 = (tile(dx, 2 - fy, 2 - fz) for dx in range(3))
                for i in range(wide):
                    at = slice(i * C, (i + 1) * C)
                    bmb[fy, at, fz * HALF : (fz + 1) * HALF] = band(i, w0, w1, w2)
                    if i == wide - 1:
                        edge = jnp.where(narrow == 0, w0[:, :128], 0.0).astype(BF16)
                    elif i == 0:
                        edge = jnp.where(narrow == 3, w2[:, :128], 0.0).astype(BF16)
                    else:
                        edge = none
                    beb[fy, at, fz * 128 : (fz + 1) * 128] = edge

    forward_bands()

    for p in range(2):
        for side, d in ((0, -1), (1, 1)):
            @pl.when(jnp.logical_not(exists((d, 0))))
            def _(p=p, side=side):
                hx[p, side] = jnp.zeros((COLS // 4, 128), BF16)

            @pl.when(jnp.logical_not(exists((0, d))))
            def _(p=p, side=side):
                hy[p, side] = jnp.zeros((SIDE, LANES), BF16)

            for side2, d2 in ((0, -1), (1, 1)):
                @pl.when(jnp.logical_not(exists((d, d2))))
                def _(p=p, side=side, side2=side2):
                    hc[p, side, side2] = jnp.zeros((SIDE, 128), BF16)
    for b in range(2):
        xm[b, 0:SIDE, :] = jnp.zeros((SIDE, 3 * HALF), BF16)
        xm[b, COLS + SIDE : COLS + 2 * SIDE, :] = jnp.zeros((SIDE, 3 * HALF), BF16)

    row = lax.broadcasted_iota(jnp.int32, (COLS, CAP), 0)

    def mask(d, q, val):
        hi = jnp.broadcast_to(gotv[d] >> 8, (C, CAP))
        for x in range(SIDE):
            r0 = q * LANES + x * C
            masked[d, r0 : r0 + C, :] = jnp.where(hi == x, val, 0.0).astype(BF16)

    def pool_feats(d):
        hot[d] = jnp.where(row == (gotv[d] & (COLS - 1)), 1.0, 0.0).astype(BF16)
        mask(d, 0, gotf[d].astype(F32))
        mask(d, 1, 1.0)
        term = nt(hot[d], masked[d, 0 : 2 * LANES, :])
        if d == 0:
            sums[...] = term
        else:
            sums[...] += term

    def pool_cots(d):
        mask(d, 2, gotc[d].astype(F32))
        term = nt(hot[d], masked[d, 2 * LANES :, :])
        if d == 0:
            gy[...] = term
        else:
            gy[...] += term

    pool_feats(0)
    for d in range(1, n):
        copy_v(d).wait_recv()
        copy_f(d).wait_recv()
        pool_feats(d)

    count = jnp.maximum(sums[:, LANES:], 1.0)
    div[...] = count
    mean = (sums[:, :LANES] / count).astype(BF16)

    def shifts(val):
        z = lax.broadcasted_iota(jnp.int32, val.shape, 0) & (SIDE - 1)
        down = jnp.where(z == 0, 0.0, pltpu.roll(val, 1, 0))
        up = jnp.where(z == SIDE - 1, 0.0, pltpu.roll(val, val.shape[0] - 1, 0))
        return down.astype(BF16), val.astype(BF16), up.astype(BF16)

    lane = lax.broadcasted_iota(jnp.int32, (COLS // 4, 128), 1) // C

    def pack(val, at):
        whole = None
        for q in range(4):
            part = val[q * (COLS // 4) : (q + 1) * (COLS // 4), :]
            if q != at:
                part = pltpu.roll(part, (q - at) % 4 * C, 1)
            whole = part if whole is None else jnp.where(lane == q, part, whole)
        return whole.astype(BF16)

    def unpack(val, at):
        val = val.astype(F32)
        return jnp.concatenate(
            [val if q == at else pltpu.roll(val, (at - q) % 4 * C, 1) for q in range(4)], axis=0)

    def halo(p, k):
        dx, dy = WAYS[k]
        src_rows = pl.ds(0, SIDE) if dy < 0 else pl.ds(COLS - SIDE, SIDE)
        if dx == 0:
            src = inner.at[p, src_rows, :]
            dst = hy.at[p, 0 if dy > 0 else 1]
        elif dy == 0:
            src = packed.at[p, 0 if dx < 0 else 1]
            dst = hx.at[p, 0 if dx > 0 else 1]
        else:
            src = inner.at[p, src_rows, pl.ds(0 if dx < 0 else LANES - 128, 128)]
            dst = hc.at[p, 0 if dx > 0 else 1, 0 if dy > 0 else 1]
        return pltpu.make_async_remote_copy(
            src_ref=src, dst_ref=dst, send_sem=hs.at[p, k], recv_sem=hr.at[p, k],
            device_id=(s + dx, g + dy), device_id_type=MESH)

    def convolve(p, val, main, edges, dot, meanwhile):
        inner[p] = val
        packed[p, 0] = pack(val[:, 0:128].astype(F32), 0)
        packed[p, 1] = pack(val[:, LANES - 128 :].astype(F32), 3)
        for k, w in enumerate(WAYS):
            @pl.when(exists(w))
            def _(k=k):
                halo(p, k).start()
        for b in range(2):
            for j, part in enumerate(shifts(val[:, b * HALF : (b + 1) * HALF].astype(F32))):
                xm[b, SIDE : SIDE + COLS, j * HALF : (j + 1) * HALF] = part
        total = None
        for dy in range(3):
            lhs = xm[:, dy * SIDE : dy * SIDE + COLS, :].reshape(2 * COLS, 3 * HALF)
            term = dot(lhs, main[dy])
            total = term if total is None else total + term
        acc[...] = total.reshape(2, COLS, HALF)
        meanwhile()
        for k, w in enumerate(WAYS):
            @pl.when(exists((-w[0], -w[1])))
            def _(k=k):
                halo(p, k).wait_recv()
        for side in range(2):
            rim = hy[p, side].astype(F32)
            for b in range(2):
                for j, part in enumerate(shifts(rim[:, b * HALF : (b + 1) * HALF])):
                    xh[side, b, :, j * HALF : (j + 1) * HALF] = part
        span = COLS + 2 * SIDE
        first = lax.broadcasted_iota(jnp.int32, (span, 128), 1) < C
        for b in range(2):
            at = slice(HALF, HALF + 128) if b == 0 else slice(HALF - 128, HALF)
            own = jnp.concatenate([hy[p, 0, :, at], inner[p, :, at], hy[p, 1, :, at]], axis=0).astype(F32)
            far = jnp.concatenate(
                [hc[p, b, 0].astype(F32), unpack(hx[p, b], 0 if b else 3), hc[p, b, 1].astype(F32)], axis=0)
            edge = jnp.where(first, own, far) if b == 0 else jnp.where(first, far, own)
            for j, part in enumerate(shifts(edge)):
                xe[b, :, j * 128 : (j + 1) * 128] = part
        total = None
        for dy in range(3):
            lhs = xe[:, dy * SIDE : dy * SIDE + COLS, :].reshape(2 * COLS, 3 * 128)
            term = dot(lhs, edges[dy])
            total = term if total is None else total + term
        acc[...] += total.reshape(2, COLS, HALF)
        for side, dy, r0 in ((0, 0, 0), (1, 2, COLS - SIDE)):
            term = dot(xh[side].reshape(2 * SIDE, 3 * HALF), main[dy])
            acc[:, r0 : r0 + SIDE, :] += term.reshape(2, SIDE, HALF)

    def first_wait():
        for d in range(n):
            if d:
                copy_c(d).wait_recv()
            pool_cots(d)
        backward_bands()

    convolve(0, mean, bmf, bef, nn, first_wait)
    parts = []
    for b in range(2):
        o = acc[b]
        sig = 1.0 / (1.0 + jnp.exp(-o))
        parts.append((gy[:, b * HALF : (b + 1) * HALF] * sig * (1.0 + o * (1.0 - sig))).astype(BF16))
    convolve(1, jnp.concatenate(parts, axis=1), bmb, beb, nt, lambda: None)

    grad = jnp.concatenate([acc[b] / div[:, b * HALF : (b + 1) * HALF] for b in range(2)], axis=1)
    grad = jnp.transpose(grad).astype(BF16)

    def copy_r(d):
        return pltpu.make_async_remote_copy(
            src_ref=back.at[d], dst_ref=out.at[:, slots_of(g)], send_sem=rs.at[d], recv_sem=rr.at[d],
            device_id=(s, peer(n - d)), device_id_type=MESH)

    for d in list(range(1, n)) + [0]:
        hi = jnp.broadcast_to(gotv[d] >> 8, (C, CAP))
        rows = nn(grad, hot[d])
        picked = jnp.zeros((C, CAP), F32)
        for x in range(SIDE):
            picked = picked + jnp.where(hi == x, rows[x * C : (x + 1) * C], 0.0)
        if d == 0:
            out[:, slots_of(g)] = picked.astype(BF16)
        else:
            back[d] = picked.astype(BF16)
            copy_r(d).start()
    for d in range(1, n):
        copy_r(d).wait_recv()
    for d in range(1, n):
        copy_v(d).wait_send()
        copy_f(d).wait_send()
        copy_c(d).wait_send()
        copy_r(d).wait_send()
    for p in range(2):
        for k, w in enumerate(WAYS):
            @pl.when(exists(w))
            def _(p=p, k=k):
                halo(p, k).wait_send()


def per_device(n, ns, point_feats, point_voxel, cotangent, weights):
    slots = n * CAP
    span = COLS + 2 * SIDE
    vm = pltpu.VMEM
    dma = pltpu.SemaphoreType.DMA
    return pl.pallas_call(
        functools.partial(kernel, n, ns),
        out_shape=jax.ShapeDtypeStruct((C, slots), BF16),
        in_specs=[pl.BlockSpec(memory_space=pltpu.HBM)] * 4,
        out_specs=pl.BlockSpec(memory_space=vm),
        scratch_shapes=[
            vm((n, C, CAP), BF16),
            vm((n, C, CAP), BF16),
            vm((n, 1, CAP), jnp.int32),
            vm((27 * C, C), BF16),
            vm((n, COLS, CAP), BF16),
            vm((n, 3 * LANES, CAP), BF16),
            vm((COLS, 2 * LANES), F32),
            vm((27 * C, HALF), F32),
            vm((3, 3 * HALF, HALF), BF16),
            vm((3, 3 * 128, HALF), BF16),
            vm((3, HALF, 3 * HALF), BF16),
            vm((3, HALF, 3 * 128), BF16),
            vm((2, COLS, LANES), BF16),
            vm((2, 2, COLS // 4, 128), BF16),
            vm((2, 2, COLS // 4, 128), BF16),
            vm((2, 2, 2, SIDE, 128), BF16),
            vm((2, 2, SIDE, LANES), BF16),
            vm((2, span, 3 * HALF), BF16),
            vm((2, span, 3 * 128), BF16),
            vm((2, 2, SIDE, 3 * HALF), BF16),
            vm((2, COLS, HALF), F32),
            vm((COLS, LANES), F32),
            vm((COLS, LANES), F32),
            vm((n, C, CAP), BF16),
            dma((4,)), dma((n,)), dma((n,)), dma((n,)), dma((n,)), dma((n,)), dma((n,)),
            dma((2, 8)), dma((2, 8)), dma((n,)), dma((n,)),
        ],
        compiler_params=pltpu.CompilerParams(
            collective_id=0, has_side_effects=True, vmem_limit_bytes=48 * 2**20
        ),
    )(point_feats.T, cotangent.T, point_voxel.reshape(n, 1, CAP), weights.reshape(27 * C, C)).T


def solution(mesh):
    n, ns = mesh.shape["group"], mesh.shape["space"]
    placed = (P(("space", "group"), None), P(("space", "group")), P(("space", "group"), None), P())
    return jax.shard_map(
        functools.partial(per_device, n, ns),
        mesh=mesh,
        in_specs=placed,
        out_specs=P(("space", "group"), None),
        check_vma=False,
    )
```

```python
import functools

import jax
import jax.numpy as jnp
from jax import lax
from jax.experimental import pallas as pl
from jax.experimental.pallas import tpu as pltpu
from jax.sharding import PartitionSpec as P

MESH = pl.DeviceIdType.MESH
F32 = jnp.float32
BF16 = jnp.bfloat16
SIDE = 16
C = 32
COLS = SIDE * SIDE
LANES = SIDE * C
HALF = LANES // 2
CAP = 256

WAYS = ((-1, 0), (1, 0), (0, -1), (0, 1), (-1, -1), (-1, 1), (1, -1), (1, 1))


def nt(a, b):
    return lax.dot_general(a, b, (((1,), (1,)), ((), ())), preferred_element_type=F32)


def nn(a, b):
    return jnp.dot(a, b, preferred_element_type=F32)


def kernel(
    n, ns, feats, cots, vox, weights, out,
    gotf, gotc, gotv, w_in, hot, masked, sums, tiled, bmf, bef, bmb, beb,
    inner, packed, hx, hc, hy, xm, xe, xh, xs, acc, gy, div, back,
    local, fs, fr, cs, cr, vs, vr, hs, hr, rs, rr,
):
    s = lax.axis_index("space")
    g = lax.axis_index("group")

    def exists(way):
        ok = None
        for d, at, size in ((way[0], s, ns), (way[1], g, n)):
            if d == 0:
                continue
            here = at > 0 if d < 0 else at < size - 1
            ok = here if ok is None else jnp.logical_and(ok, here)
        return ok

    def peer(d):
        return lax.rem(g + d, n)

    def slots_of(k):
        return pl.ds(pl.multiple_of(k * CAP, CAP), CAP)

    own_copies = [
        pltpu.make_async_copy(src, dst, local.at[i])
        for i, (src, dst) in enumerate((
            (weights, w_in), (vox.at[g], gotv.at[0]),
            (feats.at[:, slots_of(g)], gotf.at[0]), (cots.at[:, slots_of(g)], gotc.at[0])))
    ]
    for c in own_copies:
        c.start()

    barrier = pltpu.get_barrier_semaphore()
    outer = [w for w in WAYS if w[0] != 0]
    for d in range(1, n):
        pl.semaphore_signal(barrier, inc=1, device_id=(s, peer(d)), device_id_type=MESH)
    for w in outer:
        @pl.when(exists(w))
        def _(w=w):
            pl.semaphore_signal(barrier, inc=1, device_id=(s + w[0], g + w[1]), device_id_type=MESH)

    peers = n - 1
    for w in outer:
        peers = peers + jnp.where(exists(w), 1, 0)
    pl.semaphore_wait(barrier, peers)

    def copy_v(d):
        return pltpu.make_async_remote_copy(
            src_ref=vox.at[peer(d)], dst_ref=gotv.at[d], send_sem=vs.at[d], recv_sem=vr.at[d],
            device_id=(s, peer(d)), device_id_type=MESH)

    def copy_f(d):
        return pltpu.make_async_remote_copy(
            src_ref=feats.at[:, slots_of(peer(d))], dst_ref=gotf.at[d], send_sem=fs.at[d], recv_sem=fr.at[d],
            device_id=(s, peer(d)), device_id_type=MESH)

    def copy_c(d):
        return pltpu.make_async_remote_copy(
            src_ref=cots.at[:, slots_of(peer(d))], dst_ref=gotc.at[d], send_sem=cs.at[d], recv_sem=cr.at[d],
            device_id=(s, peer(d)), device_id_type=MESH)

    for d in range(1, n):
        copy_v(d).start()
        copy_f(d).start()
    for d in range(1, n):
        copy_c(d).start()
    for c in own_copies:
        c.wait()

    spread = jnp.where(
        (lax.broadcasted_iota(jnp.int32, (C, HALF), 1) & (C - 1)) == lax.broadcasted_iota(jnp.int32, (C, HALF), 0),
        1.0, 0.0).astype(BF16)
    tiled[...] = nn(w_in[...], spread)
    block = lax.broadcasted_iota(jnp.int32, (C, HALF), 1) // C
    narrow = lax.broadcasted_iota(jnp.int32, (C, 128), 1) // C
    none = jnp.zeros((C, 128), BF16)
    wide = HALF // C

    def tile(dx, dy, dz):
        a = (dx * 3 + dy) * 3 + dz
        return tiled[a * C : (a + 1) * C, :]

    def band(i, w0, w1, w2):
        inside = jnp.where(block == i, w1, jnp.where(block == i - 1, w2, jnp.where(block == i + 1, w0, 0.0)))
        return inside.astype(BF16)

    def forward_bands():
        for dy in range(3):
            for dz in range(3):
                w0, w1, w2 = (tile(dx, dy, dz) for dx in range(3))
                for i in range(wide):
                    bmf[dy, dz * HALF + i * C : dz * HALF + (i + 1) * C, :] = band(i, w0, w1, w2)
                bef[dy, dz * 128 : dz * 128 + C, :] = jnp.where(block == wide - 1, w2, 0.0).astype(BF16)
                bef[dy, dz * 128 + C : dz * 128 + 3 * C, :] = jnp.zeros((2 * C, HALF), BF16)
                bef[dy, dz * 128 + 3 * C : dz * 128 + 4 * C, :] = jnp.where(block == 0, w0, 0.0).astype(BF16)

    def backward_bands():
        for fy in range(3):
            for fz in range(3):
                w0, w1, w2 = (tile(dx, 2 - fy, 2 - fz) for dx in range(3))
                for i in range(wide):
                    at = slice(i * C, (i + 1) * C)
                    bmb[fy, at, fz * HALF : (fz + 1) * HALF] = band(i, w0, w1, w2)
                    if i == wide - 1:
                        edge = jnp.where(narrow == 0, w0[:, :128], 0.0).astype(BF16)
                    elif i == 0:
                        edge = jnp.where(narrow == 3, w2[:, :128], 0.0).astype(BF16)
                    else:
                        edge = none
                    beb[fy, at, fz * 128 : (fz + 1) * 128] = edge

    forward_bands()

    for p in range(2):
        for side, d in ((0, -1), (1, 1)):
            @pl.when(jnp.logical_not(exists((d, 0))))
            def _(p=p, side=side):
                hx[p, side] = jnp.zeros((COLS // 4, 128), BF16)

            @pl.when(jnp.logical_not(exists((0, d))))
            def _(p=p, side=side):
                hy[p, side] = jnp.zeros((SIDE, LANES), BF16)

            for side2, d2 in ((0, -1), (1, 1)):
                @pl.when(jnp.logical_not(exists((d, d2))))
                def _(p=p, side=side, side2=side2):
                    hc[p, side, side2] = jnp.zeros((SIDE, 128), BF16)
    for b in range(2):
        xm[b, 0:SIDE, :] = jnp.zeros((SIDE, 3 * HALF), BF16)
        xm[b, COLS + SIDE : COLS + 2 * SIDE, :] = jnp.zeros((SIDE, 3 * HALF), BF16)
    xe[0, 0:SIDE, :] = jnp.zeros((SIDE, 3 * 128), BF16)
    xe[0, COLS + SIDE : COLS + 2 * SIDE, :] = jnp.zeros((SIDE, 3 * 128), BF16)

    row = lax.broadcasted_iota(jnp.int32, (COLS, CAP), 0)

    def mask(d, q, val):
        hi = jnp.broadcast_to(gotv[d] >> 8, (C, CAP))
        for x in range(SIDE):
            r0 = q * LANES + x * C
            masked[d, r0 : r0 + C, :] = jnp.where(hi == x, val, 0.0).astype(BF16)

    def pool_ones(d):
        hot[d] = jnp.where(row == (gotv[d] & (COLS - 1)), 1.0, 0.0).astype(BF16)
        mask(d, 1, 1.0)
        term = nt(hot[d], masked[d, LANES : 2 * LANES, :])
        if d == 0:
            div[...] = term
        else:
            div[...] += term

    def pool_feats(d):
        mask(d, 0, gotf[d].astype(F32))
        term = nt(hot[d], masked[d, 0:LANES, :])
        if d == 0:
            sums[...] = term
        else:
            sums[...] += term

    def pool_cots(d):
        mask(d, 2, gotc[d].astype(F32))
        term = nt(hot[d], masked[d, 2 * LANES :, :])
        if d == 0:
            gy[...] = term
        else:
            gy[...] += term

    pool_ones(0)
    pool_feats(0)
    for d in range(1, n):
        copy_v(d).wait_recv()
        pool_ones(d)
    for d in range(1, n):
        copy_f(d).wait_recv()
        pool_feats(d)

    count = jnp.maximum(div[...], 1.0)
    div[...] = count
    mean = (sums[...] / count).astype(BF16)

    def shifts(val):
        z = lax.broadcasted_iota(jnp.int32, val.shape, 0) & (SIDE - 1)
        down = jnp.where(z == 0, 0.0, pltpu.roll(val, 1, 0))
        up = jnp.where(z == SIDE - 1, 0.0, pltpu.roll(val, val.shape[0] - 1, 0))
        return down.astype(BF16), val.astype(BF16), up.astype(BF16)

    lane = lax.broadcasted_iota(jnp.int32, (COLS // 4, 128), 1) // C

    def pack(val, at):
        whole = None
        for q in range(4):
            part = val[q * (COLS // 4) : (q + 1) * (COLS // 4), :]
            if q != at:
                part = pltpu.roll(part, (q - at) % 4 * C, 1)
            whole = part if whole is None else jnp.where(lane == q, part, whole)
        return whole.astype(BF16)

    def unpack(val, at):
        val = val.astype(F32)
        return jnp.concatenate(
            [val if q == at else pltpu.roll(val, (at - q) % 4 * C, 1) for q in range(4)], axis=0)

    def halo(p, k):
        dx, dy = WAYS[k]
        src_rows = pl.ds(0, SIDE) if dy < 0 else pl.ds(COLS - SIDE, SIDE)
        if dx == 0:
            src = inner.at[p, src_rows, :]
            dst = hy.at[p, 0 if dy > 0 else 1]
        elif dy == 0:
            src = packed.at[p, 0 if dx < 0 else 1]
            dst = hx.at[p, 0 if dx > 0 else 1]
        else:
            src = inner.at[p, src_rows, pl.ds(0 if dx < 0 else LANES - 128, 128)]
            dst = hc.at[p, 0 if dx > 0 else 1, 0 if dy > 0 else 1]
        return pltpu.make_async_remote_copy(
            src_ref=src, dst_ref=dst, send_sem=hs.at[p, k], recv_sem=hr.at[p, k],
            device_id=(s + dx, g + dy), device_id_type=MESH)

    def convolve(p, val, main, edges, dot, meanwhile):
        inner[p] = val
        packed[p, 0] = pack(val[:, 0:128].astype(F32), 0)
        packed[p, 1] = pack(val[:, LANES - 128 :].astype(F32), 3)
        for k, w in enumerate(WAYS):
            @pl.when(exists(w))
            def _(k=k):
                halo(p, k).start()
        first = lax.broadcasted_iota(jnp.int32, (1, 128), 1) < C

        def seam(v):
            v = v[:, HALF - 128 : HALF + 128].astype(F32)
            return jnp.where(first, v[:, 128:], v[:, :128])

        for b in range(2):
            for j, part in enumerate(shifts(val[:, b * HALF : (b + 1) * HALF].astype(F32))):
                xm[b, SIDE : SIDE + COLS, j * HALF : (j + 1) * HALF] = part
        for j, part in enumerate(shifts(seam(val))):
            xe[0, SIDE : SIDE + COLS, j * 128 : (j + 1) * 128] = part
        total, inside = None, None
        for dy in range(3):
            at = slice(dy * SIDE, dy * SIDE + COLS)
            term = dot(xm[:, at, :].reshape(2 * COLS, 3 * HALF), main[dy])
            total = term if total is None else total + term
            term = dot(xe[0, at, :], edges[dy])
            inside = term if inside is None else inside + term
        acc[...] = total.reshape(2, COLS, HALF)
        acc[0, :, 128:] += inside[:, 128:]
        acc[1, :, :128] += inside[:, :128]
        meanwhile()
        for k, w in enumerate(WAYS):
            @pl.when(exists((-w[0], -w[1])))
            def _(k=k):
                halo(p, k).wait_recv()
        for side in range(2):
            rim = hy[p, side]
            for b in range(2):
                for j, part in enumerate(shifts(rim[:, b * HALF : (b + 1) * HALF].astype(F32))):
                    xh[side, b, :, j * HALF : (j + 1) * HALF] = part
            for j, part in enumerate(shifts(seam(rim))):
                xs[side, :, j * 128 : (j + 1) * 128] = part
        left, right = (
            jnp.concatenate(
                [hc[p, b, 0].astype(F32), unpack(hx[p, b], 0 if b else 3), hc[p, b, 1].astype(F32)], axis=0)
            for b in range(2))
        for j, part in enumerate(shifts(jnp.where(first, right, left))):
            xe[1, :, j * 128 : (j + 1) * 128] = part
        total = None
        for dy in range(3):
            term = dot(xe[1, dy * SIDE : dy * SIDE + COLS, :], edges[dy])
            total = term if total is None else total + term
        acc[0, :, :128] += total[:, :128]
        acc[1, :, 128:] += total[:, 128:]
        for side, dy, r0 in ((0, 0, 0), (1, 2, COLS - SIDE)):
            at = slice(r0, r0 + SIDE)
            term = dot(xh[side].reshape(2 * SIDE, 3 * HALF), main[dy])
            acc[:, at, :] += term.reshape(2, SIDE, HALF)
            term = dot(xs[side], edges[dy])
            acc[0, at, 128:] += term[:, 128:]
            acc[1, at, :128] += term[:, :128]

    def first_wait():
        for d in range(n):
            if d:
                copy_c(d).wait_recv()
            pool_cots(d)
        backward_bands()

    convolve(0, mean, bmf, bef, nn, first_wait)
    parts = []
    for b in range(2):
        o = acc[b]
        sig = 1.0 / (1.0 + jnp.exp(-o))
        parts.append((gy[:, b * HALF : (b + 1) * HALF] * sig * (1.0 + o * (1.0 - sig))).astype(BF16))
    convolve(1, jnp.concatenate(parts, axis=1), bmb, beb, nt, lambda: None)

    grad = jnp.concatenate([acc[b] / div[:, b * HALF : (b + 1) * HALF] for b in range(2)], axis=1)
    grad = jnp.transpose(grad).astype(BF16)

    def copy_r(d):
        return pltpu.make_async_remote_copy(
            src_ref=back.at[d], dst_ref=out.at[:, slots_of(g)], send_sem=rs.at[d], recv_sem=rr.at[d],
            device_id=(s, peer(n - d)), device_id_type=MESH)

    for d in list(range(1, n)) + [0]:
        hi = jnp.broadcast_to(gotv[d] >> 8, (C, CAP))
        rows = nn(grad, hot[d])
        picked = jnp.zeros((C, CAP), F32)
        for x in range(SIDE):
            picked = picked + jnp.where(hi == x, rows[x * C : (x + 1) * C], 0.0)
        if d == 0:
            out[:, slots_of(g)] = picked.astype(BF16)
        else:
            back[d] = picked.astype(BF16)
            copy_r(d).start()
    for d in range(1, n):
        copy_r(d).wait_recv()
    for d in range(1, n):
        copy_v(d).wait_send()
        copy_f(d).wait_send()
        copy_c(d).wait_send()
        copy_r(d).wait_send()
    for p in range(2):
        for k, w in enumerate(WAYS):
            @pl.when(exists(w))
            def _(p=p, k=k):
                halo(p, k).wait_send()


def per_device(n, ns, point_feats, point_voxel, cotangent, weights):
    slots = n * CAP
    span = COLS + 2 * SIDE
    vm = pltpu.VMEM
    dma = pltpu.SemaphoreType.DMA
    return pl.pallas_call(
        functools.partial(kernel, n, ns),
        out_shape=jax.ShapeDtypeStruct((C, slots), BF16),
        in_specs=[pl.BlockSpec(memory_space=pltpu.HBM)] * 4,
        out_specs=pl.BlockSpec(memory_space=vm),
        scratch_shapes=[
            vm((n, C, CAP), BF16),
            vm((n, C, CAP), BF16),
            vm((n, 1, CAP), jnp.int32),
            vm((27 * C, C), BF16),
            vm((n, COLS, CAP), BF16),
            vm((n, 3 * LANES, CAP), BF16),
            vm((COLS, LANES), F32),
            vm((27 * C, HALF), F32),
            vm((3, 3 * HALF, HALF), BF16),
            vm((3, 3 * 128, HALF), BF16),
            vm((3, HALF, 3 * HALF), BF16),
            vm((3, HALF, 3 * 128), BF16),
            vm((2, COLS, LANES), BF16),
            vm((2, 2, COLS // 4, 128), BF16),
            vm((2, 2, COLS // 4, 128), BF16),
            vm((2, 2, 2, SIDE, 128), BF16),
            vm((2, 2, SIDE, LANES), BF16),
            vm((2, span, 3 * HALF), BF16),
            vm((2, span, 3 * 128), BF16),
            vm((2, 2, SIDE, 3 * HALF), BF16),
            vm((2, SIDE, 3 * 128), BF16),
            vm((2, COLS, HALF), F32),
            vm((COLS, LANES), F32),
            vm((COLS, LANES), F32),
            vm((n, C, CAP), BF16),
            dma((4,)), dma((n,)), dma((n,)), dma((n,)), dma((n,)), dma((n,)), dma((n,)),
            dma((2, 8)), dma((2, 8)), dma((n,)), dma((n,)),
        ],
        compiler_params=pltpu.CompilerParams(
            collective_id=0, has_side_effects=True, vmem_limit_bytes=63 * 2**20
        ),
    )(point_feats.T, cotangent.T, point_voxel.reshape(n, 1, CAP), weights.reshape(27 * C, C)).T


def solution(mesh):
    n, ns = mesh.shape["group"], mesh.shape["space"]
    placed = (P(("space", "group"), None), P(("space", "group")), P(("space", "group"), None), P())
    return jax.shard_map(
        functools.partial(per_device, n, ns),
        mesh=mesh,
        in_specs=placed,
        out_specs=P(("space", "group"), None),
        check_vma=False,
    )
```

```python
import functools

import jax
import jax.numpy as jnp
from jax import lax
from jax.experimental import pallas as pl
from jax.experimental.pallas import tpu as pltpu
from jax.sharding import PartitionSpec as P

MESH = pl.DeviceIdType.MESH
F32 = jnp.float32
BF16 = jnp.bfloat16
SIDE = 16
C = 32
COLS = SIDE * SIDE
LANES = SIDE * C
HALF = LANES // 2
CAP = 256

WAYS = ((-1, 0), (1, 0), (0, -1), (0, 1), (-1, -1), (-1, 1), (1, -1), (1, 1))


def nt(a, b):
    return lax.dot_general(a, b, (((1,), (1,)), ((), ())), preferred_element_type=F32)


def nn(a, b):
    return jnp.dot(a, b, preferred_element_type=F32)


def kernel(
    n, ns, feats, cots, vox, weights, out,
    gotf, gotc, gotv, w_in, hot, masked, sums, tiled, bmf, bef, bmb, beb,
    inner, packed, hx, hc, hy, xm, xe, xh, xs, acc, gy, div, back,
    local, fs, fr, cs, cr, vs, vr, hs, hr, rs, rr,
):
    s = lax.axis_index("space")
    g = lax.axis_index("group")

    def exists(way):
        ok = None
        for d, at, size in ((way[0], s, ns), (way[1], g, n)):
            if d == 0:
                continue
            here = at > 0 if d < 0 else at < size - 1
            ok = here if ok is None else jnp.logical_and(ok, here)
        return ok

    def peer(d):
        return lax.rem(g + d, n)

    def slots_of(k):
        return pl.ds(pl.multiple_of(k * CAP, CAP), CAP)

    own_copies = [
        pltpu.make_async_copy(src, dst, local.at[i])
        for i, (src, dst) in enumerate((
            (weights, w_in), (vox.at[g], gotv.at[0]),
            (feats.at[:, slots_of(g)], gotf.at[0]), (cots.at[:, slots_of(g)], gotc.at[0])))
    ]
    for c in own_copies:
        c.start()

    barrier = pltpu.get_barrier_semaphore()
    outer = [w for w in WAYS if w[0] != 0]
    for d in range(1, n):
        pl.semaphore_signal(barrier, inc=1, device_id=(s, peer(d)), device_id_type=MESH)
    for w in outer:
        @pl.when(exists(w))
        def _(w=w):
            pl.semaphore_signal(barrier, inc=1, device_id=(s + w[0], g + w[1]), device_id_type=MESH)

    for p in range(2):
        for side, d in ((0, -1), (1, 1)):
            @pl.when(jnp.logical_not(exists((d, 0))))
            def _(p=p, side=side):
                hx[p, side] = jnp.zeros((COLS // 4, 128), BF16)

            @pl.when(jnp.logical_not(exists((0, d))))
            def _(p=p, side=side):
                hy[p, side] = jnp.zeros((SIDE, LANES), BF16)

            for side2, d2 in ((0, -1), (1, 1)):
                @pl.when(jnp.logical_not(exists((d, d2))))
                def _(p=p, side=side, side2=side2):
                    hc[p, side, side2] = jnp.zeros((SIDE, 128), BF16)
    for b in range(2):
        xm[b, 0:SIDE, :] = jnp.zeros((SIDE, 3 * HALF), BF16)
        xm[b, COLS + SIDE : COLS + 2 * SIDE, :] = jnp.zeros((SIDE, 3 * HALF), BF16)
    xe[0, 0:SIDE, :] = jnp.zeros((SIDE, 3 * 128), BF16)
    xe[0, COLS + SIDE : COLS + 2 * SIDE, :] = jnp.zeros((SIDE, 3 * 128), BF16)

    for dy in range(3):
        for dz in range(3):
            bef[dy, dz * 128 + C : dz * 128 + 3 * C, :] = jnp.zeros((2 * C, HALF), BF16)

    peers = n - 1
    for w in outer:
        peers = peers + jnp.where(exists(w), 1, 0)
    pl.semaphore_wait(barrier, peers)

    def copy_v(d):
        return pltpu.make_async_remote_copy(
            src_ref=vox.at[peer(d)], dst_ref=gotv.at[d], send_sem=vs.at[d], recv_sem=vr.at[d],
            device_id=(s, peer(d)), device_id_type=MESH)

    def copy_f(d):
        return pltpu.make_async_remote_copy(
            src_ref=feats.at[:, slots_of(peer(d))], dst_ref=gotf.at[d], send_sem=fs.at[d], recv_sem=fr.at[d],
            device_id=(s, peer(d)), device_id_type=MESH)

    def copy_c(d):
        return pltpu.make_async_remote_copy(
            src_ref=cots.at[:, slots_of(peer(d))], dst_ref=gotc.at[d], send_sem=cs.at[d], recv_sem=cr.at[d],
            device_id=(s, peer(d)), device_id_type=MESH)

    for d in range(1, n):
        copy_v(d).start()
        copy_f(d).start()
    for d in range(1, n):
        copy_c(d).start()
    for c in own_copies:
        c.wait()

    spread = jnp.where(
        (lax.broadcasted_iota(jnp.int32, (C, HALF), 1) & (C - 1)) == lax.broadcasted_iota(jnp.int32, (C, HALF), 0),
        1.0, 0.0).astype(BF16)
    tiled[...] = nn(w_in[...], spread)
    block = lax.broadcasted_iota(jnp.int32, (C, HALF), 1) // C
    narrow = lax.broadcasted_iota(jnp.int32, (C, 128), 1) // C
    none = jnp.zeros((C, 128), BF16)
    wide = HALF // C

    def tile(dx, dy, dz):
        a = (dx * 3 + dy) * 3 + dz
        return tiled[a * C : (a + 1) * C, :]

    def band(i, w0, w1, w2):
        inside = jnp.where(block == i, w1, jnp.where(block == i - 1, w2, jnp.where(block == i + 1, w0, 0.0)))
        return inside.astype(BF16)

    def forward_bands():
        for dy in range(3):
            for dz in range(3):
                w0, w1, w2 = (tile(dx, dy, dz) for dx in range(3))
                for i in range(wide):
                    bmf[dy, dz * HALF + i * C : dz * HALF + (i + 1) * C, :] = band(i, w0, w1, w2)
                bef[dy, dz * 128 : dz * 128 + C, :] = jnp.where(block == wide - 1, w2, 0.0).astype(BF16)
                bef[dy, dz * 128 + 3 * C : dz * 128 + 4 * C, :] = jnp.where(block == 0, w0, 0.0).astype(BF16)

    def backward_bands():
        for fy in range(3):
            for fz in range(3):
                w0, w1, w2 = (tile(dx, 2 - fy, 2 - fz) for dx in range(3))
                for i in range(wide):
                    at = slice(i * C, (i + 1) * C)
                    bmb[fy, at, fz * HALF : (fz + 1) * HALF] = band(i, w0, w1, w2)
                    if i == wide - 1:
                        edge = jnp.where(narrow == 0, w0[:, :128], 0.0).astype(BF16)
                    elif i == 0:
                        edge = jnp.where(narrow == 3, w2[:, :128], 0.0).astype(BF16)
                    else:
                        edge = none
                    beb[fy, at, fz * 128 : (fz + 1) * 128] = edge

    forward_bands()

    row = lax.broadcasted_iota(jnp.int32, (COLS, CAP), 0)

    def mask(d, q, val):
        hi = jnp.broadcast_to(gotv[d] >> 8, (C, CAP))
        for x in range(SIDE):
            r0 = q * LANES + x * C
            masked[d, r0 : r0 + C, :] = jnp.where(hi == x, val, 0.0).astype(BF16)

    def pool_ones(d):
        hot[d] = jnp.where(row == (gotv[d] & (COLS - 1)), 1.0, 0.0).astype(BF16)
        mask(d, 1, 1.0)
        term = nt(hot[d], masked[d, LANES : 2 * LANES, :])
        if d == 0:
            div[...] = term
        else:
            div[...] += term

    def pool_feats(d):
        mask(d, 0, gotf[d].astype(F32))
        term = nt(hot[d], masked[d, 0:LANES, :])
        if d == 0:
            sums[...] = term
        else:
            sums[...] += term

    def pool_cots(d):
        mask(d, 2, gotc[d].astype(F32))
        term = nt(hot[d], masked[d, 2 * LANES :, :])
        if d == 0:
            gy[...] = term
        else:
            gy[...] += term

    pool_ones(0)
    pool_feats(0)
    for d in range(1, n):
        copy_v(d).wait_recv()
        pool_ones(d)
    div[...] = 1.0 / jnp.maximum(div[...], 1.0)
    for d in range(1, n):
        copy_f(d).wait_recv()
        pool_feats(d)

    inner[0] = (sums[...] * div[...]).astype(BF16)

    def shifts(val):
        z = lax.broadcasted_iota(jnp.int32, val.shape, 0) & (SIDE - 1)
        down = jnp.where(z == 0, 0.0, pltpu.roll(val, 1, 0))
        up = jnp.where(z == SIDE - 1, 0.0, pltpu.roll(val, val.shape[0] - 1, 0))
        return down.astype(BF16), val.astype(BF16), up.astype(BF16)

    lane = lax.broadcasted_iota(jnp.int32, (COLS // 4, 128), 1) // C

    def pack(val, at):
        whole = None
        for q in range(4):
            part = val[q * (COLS // 4) : (q + 1) * (COLS // 4), :]
            if q != at:
                part = pltpu.roll(part, (q - at) % 4 * C, 1)
            whole = part if whole is None else jnp.where(lane == q, part, whole)
        return whole.astype(BF16)

    def unpack(val, at):
        val = val.astype(F32)
        return jnp.concatenate(
            [val if q == at else pltpu.roll(val, (at - q) % 4 * C, 1) for q in range(4)], axis=0)

    def halo(p, k):
        dx, dy = WAYS[k]
        src_rows = pl.ds(0, SIDE) if dy < 0 else pl.ds(COLS - SIDE, SIDE)
        if dx == 0:
            src = inner.at[p, src_rows, :]
            dst = hy.at[p, 0 if dy > 0 else 1]
        elif dy == 0:
            src = packed.at[p, 0 if dx < 0 else 1]
            dst = hx.at[p, 0 if dx > 0 else 1]
        else:
            src = inner.at[p, src_rows, pl.ds(0 if dx < 0 else LANES - 128, 128)]
            dst = hc.at[p, 0 if dx > 0 else 1, 0 if dy > 0 else 1]
        return pltpu.make_async_remote_copy(
            src_ref=src, dst_ref=dst, send_sem=hs.at[p, k], recv_sem=hr.at[p, k],
            device_id=(s + dx, g + dy), device_id_type=MESH)

    def convolve(p, main, edges, dot, meanwhile):
        val = inner[p]
        packed[p, 0] = pack(val[:, 0:128].astype(F32), 0)
        packed[p, 1] = pack(val[:, LANES - 128 :].astype(F32), 3)
        for k, w in enumerate(WAYS):
            @pl.when(exists(w))
            def _(k=k):
                halo(p, k).start()
        first = lax.broadcasted_iota(jnp.int32, (1, 128), 1) < C

        def seam(v):
            v = v[:, HALF - 128 : HALF + 128].astype(F32)
            return jnp.where(first, v[:, 128:], v[:, :128])

        for b in range(2):
            for j, part in enumerate(shifts(val[:, b * HALF : (b + 1) * HALF].astype(F32))):
                xm[b, SIDE : SIDE + COLS, j * HALF : (j + 1) * HALF] = part
        for j, part in enumerate(shifts(seam(val))):
            xe[0, SIDE : SIDE + COLS, j * 128 : (j + 1) * 128] = part
        total, inside = None, None
        for dy in range(3):
            at = slice(dy * SIDE, dy * SIDE + COLS)
            term = dot(xm[:, at, :].reshape(2 * COLS, 3 * HALF), main[dy])
            total = term if total is None else total + term
            term = dot(xe[0, at, :], edges[dy])
            inside = term if inside is None else inside + term
        acc[...] = total.reshape(2, COLS, HALF)
        acc[0, :, 128:] += inside[:, 128:]
        acc[1, :, :128] += inside[:, :128]
        meanwhile()
        for k, w in enumerate(WAYS):
            @pl.when(exists((-w[0], -w[1])))
            def _(k=k):
                halo(p, k).wait_recv()
        for side in range(2):
            rim = hy[p, side]
            for b in range(2):
                for j, part in enumerate(shifts(rim[:, b * HALF : (b + 1) * HALF].astype(F32))):
                    xh[side, b, :, j * HALF : (j + 1) * HALF] = part
            for j, part in enumerate(shifts(seam(rim))):
                xs[side, :, j * 128 : (j + 1) * 128] = part
        left, right = (
            jnp.concatenate(
                [hc[p, b, 0].astype(F32), unpack(hx[p, b], 0 if b else 3), hc[p, b, 1].astype(F32)], axis=0)
            for b in range(2))
        for j, part in enumerate(shifts(jnp.where(first, right, left))):
            xe[1, :, j * 128 : (j + 1) * 128] = part
        total = None
        for dy in range(3):
            term = dot(xe[1, dy * SIDE : dy * SIDE + COLS, :], edges[dy])
            total = term if total is None else total + term
        acc[0, :, :128] += total[:, :128]
        acc[1, :, 128:] += total[:, 128:]
        for side, dy, r0 in ((0, 0, 0), (1, 2, COLS - SIDE)):
            at = slice(r0, r0 + SIDE)
            term = dot(xh[side].reshape(2 * SIDE, 3 * HALF), main[dy])
            acc[:, at, :] += term.reshape(2, SIDE, HALF)
            term = dot(xs[side], edges[dy])
            acc[0, at, 128:] += term[:, 128:]
            acc[1, at, :128] += term[:, :128]

    def gate(tile_no, rows):
        at = slice(tile_no * 128, (tile_no + 1) * 128)
        half = slice(tile_no % 2 * 128, (tile_no % 2 + 1) * 128)
        o = acc[tile_no // 2, rows, half]
        sig = 1.0 / (1.0 + jnp.exp(-o))
        inner[1, rows, at] = (gy[rows, at] * sig * (1.0 + o * (1.0 - sig))).astype(BF16)

    def first_wait():
        for d in range(n):
            if d:
                copy_c(d).wait_recv()
            pool_cots(d)
        for tile_no in (1, 2):
            gate(tile_no, slice(SIDE, COLS - SIDE))
        backward_bands()

    convolve(0, bmf, bef, nn, first_wait)
    for tile_no in (0, 3):
        gate(tile_no, slice(0, COLS))
    for tile_no in (1, 2):
        gate(tile_no, slice(0, SIDE))
        gate(tile_no, slice(COLS - SIDE, COLS))
    convolve(1, bmb, beb, nt, lambda: None)

    grad = jnp.concatenate([acc[b] * div[:, b * HALF : (b + 1) * HALF] for b in range(2)], axis=1)
    grad = jnp.transpose(grad).astype(BF16)

    def copy_r(d):
        return pltpu.make_async_remote_copy(
            src_ref=back.at[d], dst_ref=out.at[:, slots_of(g)], send_sem=rs.at[d], recv_sem=rr.at[d],
            device_id=(s, peer(n - d)), device_id_type=MESH)

    for d in list(range(1, n)) + [0]:
        hi = jnp.broadcast_to(gotv[d] >> 8, (C, CAP))
        rows = nn(grad, hot[d])
        picked = jnp.zeros((C, CAP), F32)
        for x in range(SIDE):
            picked = picked + jnp.where(hi == x, rows[x * C : (x + 1) * C], 0.0)
        if d == 0:
            out[:, slots_of(g)] = picked.astype(BF16)
        else:
            back[d] = picked.astype(BF16)
            copy_r(d).start()
    for d in range(1, n):
        copy_r(d).wait_recv()
    for d in range(1, n):
        copy_v(d).wait_send()
        copy_f(d).wait_send()
        copy_c(d).wait_send()
        copy_r(d).wait_send()
    for p in range(2):
        for k, w in enumerate(WAYS):
            @pl.when(exists(w))
            def _(p=p, k=k):
                halo(p, k).wait_send()


def per_device(n, ns, point_feats, point_voxel, cotangent, weights):
    slots = n * CAP
    span = COLS + 2 * SIDE
    vm = pltpu.VMEM
    dma = pltpu.SemaphoreType.DMA
    return pl.pallas_call(
        functools.partial(kernel, n, ns),
        out_shape=pltpu.VMEM((C, slots), BF16),
        in_specs=[pl.BlockSpec(memory_space=pltpu.HBM)] * 4,
        out_specs=pl.BlockSpec(memory_space=vm),
        scratch_shapes=[
            vm((n, C, CAP), BF16),
            vm((n, C, CAP), BF16),
            vm((n, 1, CAP), jnp.int32),
            vm((27 * C, C), BF16),
            vm((n, COLS, CAP), BF16),
            vm((n, 3 * LANES, CAP), BF16),
            vm((COLS, LANES), F32),
            vm((27 * C, HALF), F32),
            vm((3, 3 * HALF, HALF), BF16),
            vm((3, 3 * 128, HALF), BF16),
            vm((3, HALF, 3 * HALF), BF16),
            vm((3, HALF, 3 * 128), BF16),
            vm((2, COLS, LANES), BF16),
            vm((2, 2, COLS // 4, 128), BF16),
            vm((2, 2, COLS // 4, 128), BF16),
            vm((2, 2, 2, SIDE, 128), BF16),
            vm((2, 2, SIDE, LANES), BF16),
            vm((2, span, 3 * HALF), BF16),
            vm((2, span, 3 * 128), BF16),
            vm((2, 2, SIDE, 3 * HALF), BF16),
            vm((2, SIDE, 3 * 128), BF16),
            vm((2, COLS, HALF), F32),
            vm((COLS, LANES), F32),
            vm((COLS, LANES), F32),
            vm((n, C, CAP), BF16),
            dma((4,)), dma((n,)), dma((n,)), dma((n,)), dma((n,)), dma((n,)), dma((n,)),
            dma((2, 8)), dma((2, 8)), dma((n,)), dma((n,)),
        ],
        compiler_params=pltpu.CompilerParams(
            collective_id=0, has_side_effects=True, vmem_limit_bytes=63 * 2**20
        ),
    )(point_feats.T, cotangent.T, point_voxel.reshape(n, 1, CAP), weights.reshape(27 * C, C)).T


def solution(mesh):
    n, ns = mesh.shape["group"], mesh.shape["space"]
    placed = (P(("space", "group"), None), P(("space", "group")), P(("space", "group"), None), P())
    return jax.shard_map(
        functools.partial(per_device, n, ns),
        mesh=mesh,
        in_specs=placed,
        out_specs=P(("space", "group"), None),
        check_vma=False,
    )
```

```python
import functools

import jax
import jax.numpy as jnp
from jax import lax
from jax.experimental import pallas as pl
from jax.experimental.pallas import tpu as pltpu
from jax.sharding import PartitionSpec as P

MESH = pl.DeviceIdType.MESH
F32 = jnp.float32
BF16 = jnp.bfloat16
SIDE = 16
C = 32
COLS = SIDE * SIDE
LANES = SIDE * C
HALF = LANES // 2
CAP = 256

WAYS = ((-1, 0), (1, 0), (0, -1), (0, 1), (-1, -1), (-1, 1), (1, -1), (1, 1))


def nt(a, b):
    return lax.dot_general(a, b, (((1,), (1,)), ((), ())), preferred_element_type=F32)


def nn(a, b):
    return jnp.dot(a, b, preferred_element_type=F32)


def kernel(
    n, ns, feats, cots, vox, weights, out,
    gotf, gotc, gotv, w_in, hot, masked, sums, tiled, bmf, bef, bmb, beb,
    inner, packed, hx, hc, hy, xm, xe, xh, xf, acc, gy, div, back,
    local, fs, fr, cs, cr, vs, vr, hs, hr, rs, rr,
):
    s = lax.axis_index("space")
    g = lax.axis_index("group")

    def exists(way):
        ok = None
        for d, at, size in ((way[0], s, ns), (way[1], g, n)):
            if d == 0:
                continue
            here = at > 0 if d < 0 else at < size - 1
            ok = here if ok is None else jnp.logical_and(ok, here)
        return ok

    def peer(d):
        return lax.rem(g + d, n)

    def slots_of(k):
        return pl.ds(pl.multiple_of(k * CAP, CAP), CAP)

    own_copies = [
        pltpu.make_async_copy(src, dst, local.at[i])
        for i, (src, dst) in enumerate((
            (weights, w_in), (vox.at[g], gotv.at[0]),
            (feats.at[:, slots_of(g)], gotf.at[0]), (cots.at[:, slots_of(g)], gotc.at[0])))
    ]
    for c in own_copies:
        c.start()

    barrier = pltpu.get_barrier_semaphore()
    outer = [w for w in WAYS if w[0] != 0]
    for d in range(1, n):
        pl.semaphore_signal(barrier, inc=1, device_id=(s, peer(d)), device_id_type=MESH)
    for w in outer:
        @pl.when(exists(w))
        def _(w=w):
            pl.semaphore_signal(barrier, inc=1, device_id=(s + w[0], g + w[1]), device_id_type=MESH)

    for p in range(2):
        for side, d in ((0, -1), (1, 1)):
            @pl.when(jnp.logical_not(exists((d, 0))))
            def _(p=p, side=side):
                hx[p, side] = jnp.zeros((COLS // 4, 128), BF16)

            @pl.when(jnp.logical_not(exists((0, d))))
            def _(p=p, side=side):
                hy[p, side] = jnp.zeros((SIDE, LANES), BF16)

            for side2, d2 in ((0, -1), (1, 1)):
                @pl.when(jnp.logical_not(exists((d, d2))))
                def _(p=p, side=side, side2=side2):
                    hc[p, side, side2] = jnp.zeros((SIDE, 128), BF16)
    for b in range(2):
        xm[b, 0:SIDE, :] = jnp.zeros((SIDE, 3 * HALF), BF16)
        xm[b, COLS + SIDE : COLS + 2 * SIDE, :] = jnp.zeros((SIDE, 3 * HALF), BF16)
    xe[0:SIDE, :] = jnp.zeros((SIDE, 3 * 128), BF16)
    xe[COLS + SIDE : COLS + 2 * SIDE, :] = jnp.zeros((SIDE, 3 * 128), BF16)

    for dy in range(3):
        for dz in range(3):
            bef[dy, dz * 128 + C : dz * 128 + 3 * C, :] = jnp.zeros((2 * C, HALF), BF16)

    peers = n - 1
    for w in outer:
        peers = peers + jnp.where(exists(w), 1, 0)
    pl.semaphore_wait(barrier, peers)

    def copy_v(d):
        return pltpu.make_async_remote_copy(
            src_ref=vox.at[peer(d)], dst_ref=gotv.at[d], send_sem=vs.at[d], recv_sem=vr.at[d],
            device_id=(s, peer(d)), device_id_type=MESH)

    def copy_f(d):
        return pltpu.make_async_remote_copy(
            src_ref=feats.at[:, slots_of(peer(d))], dst_ref=gotf.at[d], send_sem=fs.at[d], recv_sem=fr.at[d],
            device_id=(s, peer(d)), device_id_type=MESH)

    def copy_c(d):
        return pltpu.make_async_remote_copy(
            src_ref=cots.at[:, slots_of(peer(d))], dst_ref=gotc.at[d], send_sem=cs.at[d], recv_sem=cr.at[d],
            device_id=(s, peer(d)), device_id_type=MESH)

    for d in range(1, n):
        copy_v(d).start()
        copy_f(d).start()
    for d in range(1, n):
        copy_c(d).start()
    for c in own_copies:
        c.wait()

    spread = jnp.where(
        (lax.broadcasted_iota(jnp.int32, (C, HALF), 1) & (C - 1)) == lax.broadcasted_iota(jnp.int32, (C, HALF), 0),
        1.0, 0.0).astype(BF16)
    tiled[...] = nn(w_in[...], spread)
    block = lax.broadcasted_iota(jnp.int32, (C, HALF), 1) // C
    narrow = lax.broadcasted_iota(jnp.int32, (C, 128), 1) // C
    none = jnp.zeros((C, 128), BF16)
    wide = HALF // C

    def tile(dx, dy, dz):
        a = (dx * 3 + dy) * 3 + dz
        return tiled[a * C : (a + 1) * C, :]

    def band(i, w0, w1, w2):
        inside = jnp.where(block == i, w1, jnp.where(block == i - 1, w2, jnp.where(block == i + 1, w0, 0.0)))
        return inside.astype(BF16)

    def forward_bands():
        for dy in range(3):
            for dz in range(3):
                w0, w1, w2 = (tile(dx, dy, dz) for dx in range(3))
                for i in range(wide):
                    bmf[dy, dz * HALF + i * C : dz * HALF + (i + 1) * C, :] = band(i, w0, w1, w2)
                bef[dy, dz * 128 : dz * 128 + C, :] = jnp.where(block == wide - 1, w2, 0.0).astype(BF16)
                bef[dy, dz * 128 + 3 * C : dz * 128 + 4 * C, :] = jnp.where(block == 0, w0, 0.0).astype(BF16)

    def backward_bands():
        for fy in range(3):
            for fz in range(3):
                w0, w1, w2 = (tile(dx, 2 - fy, 2 - fz) for dx in range(3))
                for i in range(wide):
                    at = slice(i * C, (i + 1) * C)
                    bmb[fy, at, fz * HALF : (fz + 1) * HALF] = band(i, w0, w1, w2)
                    if i == wide - 1:
                        edge = jnp.where(narrow == 0, w0[:, :128], 0.0).astype(BF16)
                    elif i == 0:
                        edge = jnp.where(narrow == 3, w2[:, :128], 0.0).astype(BF16)
                    else:
                        edge = none
                    beb[fy, at, fz * 128 : (fz + 1) * 128] = edge

    forward_bands()

    row = lax.broadcasted_iota(jnp.int32, (COLS, CAP), 0)

    def columns(d):
        return slice(d * CAP, (d + 1) * CAP)

    def mask(d, q, val):
        hi = jnp.broadcast_to(gotv[d] >> 8, (C, CAP))
        for x in range(SIDE):
            r0 = q * LANES + x * C
            masked[r0 : r0 + C, columns(d)] = jnp.where(hi == x, val, 0.0).astype(BF16)

    def ones(d):
        hot[:, columns(d)] = jnp.where(row == (gotv[d] & (COLS - 1)), 1.0, 0.0).astype(BF16)
        mask(d, 1, 1.0)

    ones(0)
    mask(0, 0, gotf[0].astype(F32))
    sums[...] = nt(hot[:, columns(0)], masked[0:LANES, columns(0)])
    for d in range(1, n):
        copy_v(d).wait_recv()
        ones(d)
    div[...] = 1.0 / jnp.maximum(nt(hot[...], masked[LANES : 2 * LANES, :]), 1.0)
    for d in range(1, n):
        copy_f(d).wait_recv()
        mask(d, 0, gotf[d].astype(F32))
    far_sums = nt(hot[:, CAP:], masked[0:LANES, CAP:])
    inner[0] = ((sums[...] + far_sums) * div[...]).astype(BF16)

    def shifts(val):
        z = lax.broadcasted_iota(jnp.int32, val.shape, 0) & (SIDE - 1)
        down = jnp.where(z == 0, 0.0, pltpu.roll(val, 1, 0))
        up = jnp.where(z == SIDE - 1, 0.0, pltpu.roll(val, val.shape[0] - 1, 0))
        return down.astype(BF16), val.astype(BF16), up.astype(BF16)

    lane = lax.broadcasted_iota(jnp.int32, (COLS // 4, 128), 1) // C

    def pack(val, at):
        whole = None
        for q in range(4):
            part = val[q * (COLS // 4) : (q + 1) * (COLS // 4), :]
            if q != at:
                part = pltpu.roll(part, (q - at) % 4 * C, 1)
            whole = part if whole is None else jnp.where(lane == q, part, whole)
        return whole.astype(BF16)

    def unpack(val, at):
        val = val.astype(F32)
        return jnp.concatenate(
            [val if q == at else pltpu.roll(val, (at - q) % 4 * C, 1) for q in range(4)], axis=0)

    def halo(p, k):
        dx, dy = WAYS[k]
        src_rows = pl.ds(0, SIDE) if dy < 0 else pl.ds(COLS - SIDE, SIDE)
        if dx == 0:
            src = inner.at[p, src_rows, :]
            dst = hy.at[p, 0 if dy > 0 else 1]
        elif dy == 0:
            src = packed.at[p, 0 if dx < 0 else 1]
            dst = hx.at[p, 0 if dx > 0 else 1]
        else:
            src = inner.at[p, src_rows, pl.ds(0 if dx < 0 else LANES - 128, 128)]
            dst = hc.at[p, 0 if dx > 0 else 1, 0 if dy > 0 else 1]
        return pltpu.make_async_remote_copy(
            src_ref=src, dst_ref=dst, send_sem=hs.at[p, k], recv_sem=hr.at[p, k],
            device_id=(s + dx, g + dy), device_id_type=MESH)

    def convolve(p, main, edges, dot, before, meanwhile):
        val = inner[p]
        packed[p, 0] = pack(val[:, 0:128].astype(F32), 0)
        packed[p, 1] = pack(val[:, LANES - 128 :].astype(F32), 3)
        for k, w in enumerate(WAYS):
            @pl.when(exists(w))
            def _(k=k):
                halo(p, k).start()
        before()
        first = lax.broadcasted_iota(jnp.int32, (1, 128), 1) < C

        def seam(v):
            v = v[:, HALF - 128 : HALF + 128].astype(F32)
            return jnp.where(first, v[:, 128:], v[:, :128])

        for b in range(2):
            for j, part in enumerate(shifts(val[:, b * HALF : (b + 1) * HALF].astype(F32))):
                xm[b, SIDE : SIDE + COLS, j * HALF : (j + 1) * HALF] = part
        for j, part in enumerate(shifts(seam(val))):
            xe[SIDE : SIDE + COLS, j * 128 : (j + 1) * 128] = part
        total, inside = None, None
        for dy in range(3):
            at = slice(dy * SIDE, dy * SIDE + COLS)
            term = dot(xm[:, at, :].reshape(2 * COLS, 3 * HALF), main[dy])
            total = term if total is None else total + term
            term = dot(xe[at, :], edges[dy])
            inside = term if inside is None else inside + term
        acc[...] = total.reshape(2, COLS, HALF)
        acc[0, :, 128:] += inside[:, 128:]
        acc[1, :, :128] += inside[:, :128]
        meanwhile()
        for k, w in enumerate(WAYS):
            @pl.when(exists((-w[0], -w[1])))
            def _(k=k):
                halo(p, k).wait_recv()
        for side in range(2):
            rim = hy[p, side]
            for b in range(2):
                for j, part in enumerate(shifts(rim[:, b * HALF : (b + 1) * HALF].astype(F32))):
                    xh[side, b, :, j * HALF : (j + 1) * HALF] = part
            for j, part in enumerate(shifts(seam(rim))):
                r0 = side * (COLS + 3 * SIDE)
                xf[r0 : r0 + SIDE, j * 128 : (j + 1) * 128] = part
        left, right = (
            jnp.concatenate(
                [hc[p, b, 0].astype(F32), unpack(hx[p, b], 0 if b else 3), hc[p, b, 1].astype(F32)], axis=0)
            for b in range(2))
        for j, part in enumerate(shifts(jnp.where(first, right, left))):
            xf[SIDE : COLS + 3 * SIDE, j * 128 : (j + 1) * 128] = part
        upper = dot(xf[0 : COLS + SIDE, :], edges[0])
        lower = dot(xf[3 * SIDE : COLS + 4 * SIDE, :], edges[2])
        total = upper[SIDE:] + dot(xf[2 * SIDE : COLS + 2 * SIDE, :], edges[1]) + lower[:COLS]
        acc[0, :, :128] += total[:, :128]
        acc[1, :, 128:] += total[:, 128:]
        for side, dy, r0, rim in ((0, 0, 0, upper[:SIDE]), (1, 2, COLS - SIDE, lower[COLS:])):
            at = slice(r0, r0 + SIDE)
            term = dot(xh[side].reshape(2 * SIDE, 3 * HALF), main[dy])
            acc[:, at, :] += term.reshape(2, SIDE, HALF)
            acc[0, at, 128:] += rim[:, 128:]
            acc[1, at, :128] += rim[:, :128]

    def gate(tile_no, rows):
        at = slice(tile_no * 128, (tile_no + 1) * 128)
        half = slice(tile_no % 2 * 128, (tile_no % 2 + 1) * 128)
        o = acc[tile_no // 2, rows, half]
        sig = 1.0 / (1.0 + jnp.exp(-o))
        inner[1, rows, at] = (gy[rows, at] * sig * (1.0 + o * (1.0 - sig))).astype(BF16)

    def first_wait():
        for d in range(n):
            if d:
                copy_c(d).wait_recv()
            mask(d, 2, gotc[d].astype(F32))
        gy[...] = nt(hot[...], masked[2 * LANES :, :])
        for tile_no in (1, 2):
            gate(tile_no, slice(SIDE, COLS - SIDE))

    convolve(0, bmf, bef, nn, lambda: None, first_wait)
    for tile_no in (0, 3):
        gate(tile_no, slice(0, COLS))
    for tile_no in (1, 2):
        gate(tile_no, slice(0, SIDE))
        gate(tile_no, slice(COLS - SIDE, COLS))
    convolve(1, bmb, beb, nt, backward_bands, lambda: None)

    grad = jnp.concatenate([acc[b] * div[:, b * HALF : (b + 1) * HALF] for b in range(2)], axis=1)
    grad = jnp.transpose(grad).astype(BF16)

    def copy_r(d):
        return pltpu.make_async_remote_copy(
            src_ref=back.at[d], dst_ref=out.at[:, slots_of(g)], send_sem=rs.at[d], recv_sem=rr.at[d],
            device_id=(s, peer(n - d)), device_id_type=MESH)

    for d in list(range(1, n)) + [0]:
        hi = jnp.broadcast_to(gotv[d] >> 8, (C, CAP))
        rows = nn(grad, hot[:, columns(d)])
        picked = jnp.zeros((C, CAP), F32)
        for x in range(SIDE):
            picked = picked + jnp.where(hi == x, rows[x * C : (x + 1) * C], 0.0)
        if d == 0:
            out[:, slots_of(g)] = picked.astype(BF16)
        else:
            back[d] = picked.astype(BF16)
            copy_r(d).start()
    for d in range(1, n):
        copy_r(d).wait_recv()
    for d in range(1, n):
        copy_v(d).wait_send()
        copy_f(d).wait_send()
        copy_c(d).wait_send()
        copy_r(d).wait_send()
    for p in range(2):
        for k, w in enumerate(WAYS):
            @pl.when(exists(w))
            def _(p=p, k=k):
                halo(p, k).wait_send()


def per_device(n, ns, point_feats, point_voxel, cotangent, weights):
    slots = n * CAP
    span = COLS + 2 * SIDE
    vm = pltpu.VMEM
    dma = pltpu.SemaphoreType.DMA
    return pl.pallas_call(
        functools.partial(kernel, n, ns),
        out_shape=pltpu.VMEM((C, slots), BF16),
        in_specs=[pl.BlockSpec(memory_space=pltpu.HBM)] * 4,
        out_specs=pl.BlockSpec(memory_space=vm),
        scratch_shapes=[
            vm((n, C, CAP), BF16),
            vm((n, C, CAP), BF16),
            vm((n, 1, CAP), jnp.int32),
            vm((27 * C, C), BF16),
            vm((COLS, slots), BF16),
            vm((3 * LANES, slots), BF16),
            vm((COLS, LANES), F32),
            vm((27 * C, HALF), F32),
            vm((3, 3 * HALF, HALF), BF16),
            vm((3, 3 * 128, HALF), BF16),
            vm((3, HALF, 3 * HALF), BF16),
            vm((3, HALF, 3 * 128), BF16),
            vm((2, COLS, LANES), BF16),
            vm((2, 2, COLS // 4, 128), BF16),
            vm((2, 2, COLS // 4, 128), BF16),
            vm((2, 2, 2, SIDE, 128), BF16),
            vm((2, 2, SIDE, LANES), BF16),
            vm((2, span, 3 * HALF), BF16),
            vm((span, 3 * 128), BF16),
            vm((2, 2, SIDE, 3 * HALF), BF16),
            vm((span + 2 * SIDE, 3 * 128), BF16),
            vm((2, COLS, HALF), F32),
            vm((COLS, LANES), F32),
            vm((COLS, LANES), F32),
            vm((n, C, CAP), BF16),
            dma((4,)), dma((n,)), dma((n,)), dma((n,)), dma((n,)), dma((n,)), dma((n,)),
            dma((2, 8)), dma((2, 8)), dma((n,)), dma((n,)),
        ],
        compiler_params=pltpu.CompilerParams(
            collective_id=0, has_side_effects=True, vmem_limit_bytes=63 * 2**20
        ),
    )(point_feats.T, cotangent.T, point_voxel.reshape(n, 1, CAP), weights.reshape(27 * C, C)).T


def solution(mesh):
    n, ns = mesh.shape["group"], mesh.shape["space"]
    placed = (P(("space", "group"), None), P(("space", "group")), P(("space", "group"), None), P())
    return jax.shard_map(
        functools.partial(per_device, n, ns),
        mesh=mesh,
        in_specs=placed,
        out_specs=P(("space", "group"), None),
        check_vma=False,
    )
```

```python
import functools

import jax
import jax.numpy as jnp
from jax import lax
from jax.experimental import pallas as pl
from jax.experimental.pallas import tpu as pltpu
from jax.sharding import PartitionSpec as P

MESH = pl.DeviceIdType.MESH
F32 = jnp.float32
BF16 = jnp.bfloat16
SIDE = 16
C = 32
COLS = SIDE * SIDE
LANES = SIDE * C
HALF = LANES // 2
CAP = 256

WAYS = ((-1, 0), (1, 0), (0, -1), (0, 1), (-1, -1), (-1, 1), (1, -1), (1, 1))

BANDS = tuple((i, h) for i in range(8) for h in range(2) if any(0 <= x < 8 and x // 4 == h for x in (i - 1, i, i + 1)))


def nt(a, b):
    return lax.dot_general(a, b, (((1,), (1,)), ((), ())), preferred_element_type=F32)


def nn(a, b):
    return jnp.dot(a, b, preferred_element_type=F32)


def kernel(
    n, ns, feats, cots, vox, weights, out,
    gotf, gotc, gotv, w_in, hot, masked, sums, tiled, bmf, bef, beb,
    inner, packed, hx, hc, hy, xm, xe, xh, xf, acc, gy, div, back,
    local, fs, fr, cs, cr, vs, vr, hs, hr, rs, rr,
):
    s = lax.axis_index("space")
    g = lax.axis_index("group")

    def exists(way):
        ok = None
        for d, at, size in ((way[0], s, ns), (way[1], g, n)):
            if d == 0:
                continue
            here = at > 0 if d < 0 else at < size - 1
            ok = here if ok is None else jnp.logical_and(ok, here)
        return ok

    def peer(d):
        return lax.rem(g + d, n)

    def slots_of(k):
        return pl.ds(pl.multiple_of(k * CAP, CAP), CAP)

    own_copies = [
        pltpu.make_async_copy(src, dst, local.at[i])
        for i, (src, dst) in enumerate((
            (weights, w_in), (vox.at[g], gotv.at[0]),
            (feats.at[:, slots_of(g)], gotf.at[0]), (cots.at[:, slots_of(g)], gotc.at[0])))
    ]
    for c in own_copies:
        c.start()

    barrier = pltpu.get_barrier_semaphore()
    outer = [w for w in WAYS if w[0] != 0]
    for d in range(1, n):
        pl.semaphore_signal(barrier, inc=1, device_id=(s, peer(d)), device_id_type=MESH)
    for w in outer:
        @pl.when(exists(w))
        def _(w=w):
            pl.semaphore_signal(barrier, inc=1, device_id=(s + w[0], g + w[1]), device_id_type=MESH)

    for p in range(2):
        for side, d in ((0, -1), (1, 1)):
            @pl.when(jnp.logical_not(exists((d, 0))))
            def _(p=p, side=side):
                hx[p, side] = jnp.zeros((COLS // 4, 128), BF16)

            @pl.when(jnp.logical_not(exists((0, d))))
            def _(p=p, side=side):
                hy[p, side] = jnp.zeros((SIDE, LANES), BF16)

            for side2, d2 in ((0, -1), (1, 1)):
                @pl.when(jnp.logical_not(exists((d, d2))))
                def _(p=p, side=side, side2=side2):
                    hc[p, side, side2] = jnp.zeros((SIDE, 128), BF16)
    for b in range(2):
        xm[b, 0:SIDE, :] = jnp.zeros((SIDE, 3 * HALF), BF16)
        xm[b, COLS + SIDE : COLS + 2 * SIDE, :] = jnp.zeros((SIDE, 3 * HALF), BF16)
    xe[0:SIDE, :] = jnp.zeros((SIDE, 3 * 128), BF16)
    xe[COLS + SIDE : COLS + 2 * SIDE, :] = jnp.zeros((SIDE, 3 * 128), BF16)

    for dy in range(3):
        for dz in range(3):
            for i in range(HALF // C):
                for h in range(2):
                    if (i, h) not in BANDS:
                        bmf[dy, dz * HALF + i * C : dz * HALF + (i + 1) * C, h * 128 : (h + 1) * 128] = jnp.zeros(
                            (C, 128), BF16)
            bef[dy, dz * 128 : (dz + 1) * 128, :128] = jnp.zeros((128, 128), BF16)
            bef[dy, dz * 128 : (dz + 1) * 128, 128:] = jnp.zeros((128, 128), BF16)
            beb[dy, C : HALF - C, dz * 128 : (dz + 1) * 128] = jnp.zeros((HALF - 2 * C, 128), BF16)

    peers = n - 1
    for w in outer:
        peers = peers + jnp.where(exists(w), 1, 0)
    pl.semaphore_wait(barrier, peers)

    def copy_v(d):
        return pltpu.make_async_remote_copy(
            src_ref=vox.at[peer(d)], dst_ref=gotv.at[d], send_sem=vs.at[d], recv_sem=vr.at[d],
            device_id=(s, peer(d)), device_id_type=MESH)

    def copy_f(d):
        return pltpu.make_async_remote_copy(
            src_ref=feats.at[:, slots_of(peer(d))], dst_ref=gotf.at[d], send_sem=fs.at[d], recv_sem=fr.at[d],
            device_id=(s, peer(d)), device_id_type=MESH)

    def copy_c(d):
        return pltpu.make_async_remote_copy(
            src_ref=cots.at[:, slots_of(peer(d))], dst_ref=gotc.at[d], send_sem=cs.at[d], recv_sem=cr.at[d],
            device_id=(s, peer(d)), device_id_type=MESH)

    for d in range(1, n):
        copy_v(d).start()
        copy_f(d).start()
    for d in range(1, n):
        copy_c(d).start()
    for c in own_copies:
        c.wait()

    block = lax.broadcasted_iota(jnp.int32, (C, 128), 1) // C
    spread = jnp.where(
        (lax.broadcasted_iota(jnp.int32, (C, 128), 1) & (C - 1)) == lax.broadcasted_iota(jnp.int32, (C, 128), 0),
        1.0, 0.0).astype(BF16)
    tiled[...] = nn(w_in[...], spread)

    def tile(dx, dy, dz):
        a = (dx * 3 + dy) * 3 + dz
        return tiled[a * C : (a + 1) * C, :]

    for dy in range(3):
        for dz in range(3):
            w0, w1, w2 = (tile(dx, dy, dz) for dx in range(3))
            for i, h in BANDS:
                piece = 0.0
                for at, w in ((i + 1, w0), (i - 1, w2), (i, w1)):
                    if at // 4 == h:
                        piece = jnp.where(block == at % 4, w, piece)
                bmf[dy, dz * HALF + i * C : dz * HALF + (i + 1) * C, h * 128 : (h + 1) * 128] = piece.astype(BF16)
            high, low = jnp.where(block == 3, w2, 0.0).astype(BF16), jnp.where(block == 0, w0, 0.0).astype(BF16)
            bef[dy, dz * 128 : dz * 128 + C, 128:] = high
            bef[dy, dz * 128 + 3 * C : dz * 128 + 4 * C, :128] = low
            at = slice((2 - dz) * 128, (3 - dz) * 128)
            beb[2 - dy, HALF - C :, at] = low
            beb[2 - dy, 0:C, at] = high

    row = lax.broadcasted_iota(jnp.int32, (COLS, CAP), 0)

    def columns(d):
        return slice(d * CAP, (d + 1) * CAP)

    def mask(d, q, val):
        hi = jnp.broadcast_to(gotv[d] >> 8, (C, CAP))
        for x in range(SIDE):
            r0 = q * LANES + x * C
            masked[r0 : r0 + C, columns(d)] = jnp.where(hi == x, val, 0.0).astype(BF16)

    def ones(d):
        hot[:, columns(d)] = jnp.where(row == (gotv[d] & (COLS - 1)), 1.0, 0.0).astype(BF16)
        mask(d, 1, 1.0)

    ones(0)
    mask(0, 0, gotf[0].astype(F32))
    sums[...] = nt(hot[:, columns(0)], masked[0:LANES, columns(0)])
    for d in range(1, n):
        copy_v(d).wait_recv()
        ones(d)
    div[...] = 1.0 / jnp.maximum(nt(hot[...], masked[LANES : 2 * LANES, :]), 1.0)
    for d in range(1, n):
        copy_f(d).wait_recv()
        mask(d, 0, gotf[d].astype(F32))
    far_sums = nt(hot[:, CAP:], masked[0:LANES, CAP:])
    inner[0] = ((sums[...] + far_sums) * div[...]).astype(BF16)

    def shifts(val):
        z = lax.broadcasted_iota(jnp.int32, val.shape, 0) & (SIDE - 1)
        down = jnp.where(z == 0, 0.0, pltpu.roll(val, 1, 0))
        up = jnp.where(z == SIDE - 1, 0.0, pltpu.roll(val, val.shape[0] - 1, 0))
        return down.astype(BF16), val.astype(BF16), up.astype(BF16)

    lane = lax.broadcasted_iota(jnp.int32, (COLS // 4, 128), 1) // C

    def pack(val, at):
        whole = None
        for q in range(4):
            part = val[q * (COLS // 4) : (q + 1) * (COLS // 4), :]
            if q != at:
                part = pltpu.roll(part, (q - at) % 4 * C, 1)
            whole = part if whole is None else jnp.where(lane == q, part, whole)
        return whole.astype(BF16)

    def unpack(val, at):
        val = val.astype(F32)
        return jnp.concatenate(
            [val if q == at else pltpu.roll(val, (at - q) % 4 * C, 1) for q in range(4)], axis=0)

    def halo(p, k):
        dx, dy = WAYS[k]
        src_rows = pl.ds(0, SIDE) if dy < 0 else pl.ds(COLS - SIDE, SIDE)
        if dx == 0:
            src = inner.at[p, src_rows, :]
            dst = hy.at[p, 0 if dy > 0 else 1]
        elif dy == 0:
            src = packed.at[p, 0 if dx < 0 else 1]
            dst = hx.at[p, 0 if dx > 0 else 1]
        else:
            src = inner.at[p, src_rows, pl.ds(0 if dx < 0 else LANES - 128, 128)]
            dst = hc.at[p, 0 if dx > 0 else 1, 0 if dy > 0 else 1]
        return pltpu.make_async_remote_copy(
            src_ref=src, dst_ref=dst, send_sem=hs.at[p, k], recv_sem=hr.at[p, k],
            device_id=(s + dx, g + dy), device_id_type=MESH)

    def convolve(p, main, edges, dot, meanwhile):
        val = inner[p]
        packed[p, 0] = pack(val[:, 0:128].astype(F32), 0)
        packed[p, 1] = pack(val[:, LANES - 128 :].astype(F32), 3)
        for k, w in enumerate(WAYS):
            @pl.when(exists(w))
            def _(k=k):
                halo(p, k).start()
        first = lax.broadcasted_iota(jnp.int32, (1, 128), 1) < C

        def seam(v):
            v = v[:, HALF - 128 : HALF + 128].astype(F32)
            return jnp.where(first, v[:, 128:], v[:, :128])

        for b in range(2):
            for j, part in enumerate(shifts(val[:, b * HALF : (b + 1) * HALF].astype(F32))):
                xm[b, SIDE : SIDE + COLS, j * HALF : (j + 1) * HALF] = part
        for j, part in enumerate(shifts(seam(val))):
            xe[SIDE : SIDE + COLS, j * 128 : (j + 1) * 128] = part
        total, inside = None, None
        for dy in range(3):
            at = slice(dy * SIDE, dy * SIDE + COLS)
            term = main(xm[:, at, :].reshape(2 * COLS, 3 * HALF), dy)
            total = term if total is None else total + term
            term = dot(xe[at, :], edges[dy])
            inside = term if inside is None else inside + term
        acc[...] = total.reshape(2, COLS, HALF)
        acc[0, :, 128:] += inside[:, 128:]
        acc[1, :, :128] += inside[:, :128]
        meanwhile()
        for k, w in enumerate(WAYS):
            @pl.when(exists((-w[0], -w[1])))
            def _(k=k):
                halo(p, k).wait_recv()
        for side in range(2):
            rim = hy[p, side]
            for b in range(2):
                for j, part in enumerate(shifts(rim[:, b * HALF : (b + 1) * HALF].astype(F32))):
                    xh[side, b, :, j * HALF : (j + 1) * HALF] = part
            for j, part in enumerate(shifts(seam(rim))):
                r0 = side * (COLS + 3 * SIDE)
                xf[r0 : r0 + SIDE, j * 128 : (j + 1) * 128] = part
        left, right = (
            jnp.concatenate(
                [hc[p, b, 0].astype(F32), unpack(hx[p, b], 0 if b else 3), hc[p, b, 1].astype(F32)], axis=0)
            for b in range(2))
        for j, part in enumerate(shifts(jnp.where(first, right, left))):
            xf[SIDE : COLS + 3 * SIDE, j * 128 : (j + 1) * 128] = part
        upper = dot(xf[0 : COLS + SIDE, :], edges[0])
        lower = dot(xf[3 * SIDE : COLS + 4 * SIDE, :], edges[2])
        total = upper[SIDE:] + dot(xf[2 * SIDE : COLS + 2 * SIDE, :], edges[1]) + lower[:COLS]
        acc[0, :, :128] += total[:, :128]
        acc[1, :, 128:] += total[:, 128:]
        for side, dy, r0, rim in ((0, 0, 0, upper[:SIDE]), (1, 2, COLS - SIDE, lower[COLS:])):
            at = slice(r0, r0 + SIDE)
            term = main(xh[side].reshape(2 * SIDE, 3 * HALF), dy)
            acc[:, at, :] += term.reshape(2, SIDE, HALF)
            acc[0, at, 128:] += rim[:, 128:]
            acc[1, at, :128] += rim[:, :128]

    def gate(tile_no, rows):
        at = slice(tile_no * 128, (tile_no + 1) * 128)
        half = slice(tile_no % 2 * 128, (tile_no % 2 + 1) * 128)
        o = acc[tile_no // 2, rows, half]
        sig = 1.0 / (1.0 + jnp.exp(-o))
        inner[1, rows, at] = (gy[rows, at] * sig * (1.0 + o * (1.0 - sig))).astype(BF16)

    def forward(lhs, dy):
        return nn(lhs, bmf[dy])

    def backward(lhs, dy):
        total = None
        for dz in range(3):
            flip = slice((2 - dz) * HALF, (3 - dz) * HALF)
            term = nt(lhs[:, dz * HALF : (dz + 1) * HALF], bmf[2 - dy, flip, :])
            total = term if total is None else total + term
        return total

    def first_wait():
        for d in range(n):
            if d:
                copy_c(d).wait_recv()
            mask(d, 2, gotc[d].astype(F32))
        gy[...] = nt(hot[...], masked[2 * LANES :, :])
        for tile_no in (1, 2):
            gate(tile_no, slice(SIDE, COLS - SIDE))

    convolve(0, forward, bef, nn, first_wait)
    for tile_no in (0, 3):
        gate(tile_no, slice(0, COLS))
    for tile_no in (1, 2):
        gate(tile_no, slice(0, SIDE))
        gate(tile_no, slice(COLS - SIDE, COLS))
    convolve(1, backward, beb, nt, lambda: None)

    grad = jnp.concatenate([acc[b] * div[:, b * HALF : (b + 1) * HALF] for b in range(2)], axis=1)
    grad = jnp.transpose(grad).astype(BF16)

    def copy_r(d):
        return pltpu.make_async_remote_copy(
            src_ref=back.at[d], dst_ref=out.at[:, slots_of(g)], send_sem=rs.at[d], recv_sem=rr.at[d],
            device_id=(s, peer(n - d)), device_id_type=MESH)

    for d in list(range(1, n)) + [0]:
        hi = jnp.broadcast_to(gotv[d] >> 8, (C, CAP))
        rows = nn(grad, hot[:, columns(d)])
        picked = jnp.zeros((C, CAP), F32)
        for x in range(SIDE):
            picked = picked + jnp.where(hi == x, rows[x * C : (x + 1) * C], 0.0)
        if d == 0:
            out[:, slots_of(g)] = picked.astype(BF16)
        else:
            back[d] = picked.astype(BF16)
            copy_r(d).start()
    for d in range(1, n):
        copy_v(d).wait_send()
        copy_f(d).wait_send()
        copy_c(d).wait_send()
    for p in range(2):
        for k, w in enumerate(WAYS):
            @pl.when(exists(w))
            def _(p=p, k=k):
                halo(p, k).wait_send()
    for d in range(1, n):
        copy_r(d).wait()


def per_device(n, ns, point_feats, point_voxel, cotangent, weights):
    slots = n * CAP
    span = COLS + 2 * SIDE
    vm = pltpu.VMEM
    dma = pltpu.SemaphoreType.DMA
    return pl.pallas_call(
        functools.partial(kernel, n, ns),
        out_shape=pltpu.VMEM((C, slots), BF16),
        in_specs=[pl.BlockSpec(memory_space=pltpu.HBM)] * 4,
        out_specs=pl.BlockSpec(memory_space=vm),
        scratch_shapes=[
            vm((n, C, CAP), BF16),
            vm((n, C, CAP), BF16),
            vm((n, 1, CAP), jnp.int32),
            vm((27 * C, C), BF16),
            vm((COLS, slots), BF16),
            vm((3 * LANES, slots), BF16),
            vm((COLS, LANES), F32),
            vm((27 * C, 128), F32),
            vm((3, 3 * HALF, HALF), BF16),
            vm((3, 3 * 128, HALF), BF16),
            vm((3, HALF, 3 * 128), BF16),
            vm((2, COLS, LANES), BF16),
            vm((2, 2, COLS // 4, 128), BF16),
            vm((2, 2, COLS // 4, 128), BF16),
            vm((2, 2, 2, SIDE, 128), BF16),
            vm((2, 2, SIDE, LANES), BF16),
            vm((2, span, 3 * HALF), BF16),
            vm((span, 3 * 128), BF16),
            vm((2, 2, SIDE, 3 * HALF), BF16),
            vm((span + 2 * SIDE, 3 * 128), BF16),
            vm((2, COLS, HALF), F32),
            vm((COLS, LANES), F32),
            vm((COLS, LANES), F32),
            vm((n, C, CAP), BF16),
            dma((4,)), dma((n,)), dma((n,)), dma((n,)), dma((n,)), dma((n,)), dma((n,)),
            dma((2, 8)), dma((2, 8)), dma((n,)), dma((n,)),
        ],
        compiler_params=pltpu.CompilerParams(
            collective_id=0, has_side_effects=True, vmem_limit_bytes=63 * 2**20
        ),
    )(point_feats.T, cotangent.T, point_voxel.reshape(n, 1, CAP), weights.reshape(27 * C, C)).T


def solution(mesh):
    n, ns = mesh.shape["group"], mesh.shape["space"]
    placed = (P(("space", "group"), None), P(("space", "group")), P(("space", "group"), None), P())
    return jax.shard_map(
        functools.partial(per_device, n, ns),
        mesh=mesh,
        in_specs=placed,
        out_specs=P(("space", "group"), None),
        check_vma=False,
    )
```

```python
import functools

import jax
import jax.numpy as jnp
from jax import lax
from jax.experimental import pallas as pl
from jax.experimental.pallas import tpu as pltpu
from jax.sharding import PartitionSpec as P

MESH = pl.DeviceIdType.MESH
F32 = jnp.float32
BF16 = jnp.bfloat16
SIDE = 16
C = 32
COLS = SIDE * SIDE
LANES = SIDE * C
HALF = LANES // 2
CAP = 256

WAYS = ((-1, -1), (-1, 1), (1, -1), (1, 1), (-1, 0), (1, 0), (0, -1), (0, 1))

BANDS = tuple((i, h) for i in range(8) for h in range(2) if any(0 <= x < 8 and x // 4 == h for x in (i - 1, i, i + 1)))


def nt(a, b):
    return lax.dot_general(a, b, (((1,), (1,)), ((), ())), preferred_element_type=F32)


def nn(a, b):
    return jnp.dot(a, b, preferred_element_type=F32)


def kernel(
    n, ns, feats, cots, vox, weights, out,
    gotf, gotc, gotv, w_in, hot, masked, sums, tiled, bmf, bef, beb,
    inner, packed, hx, hc, hy, xm, xe, xh, xf, acc, gy, div, back,
    local, fs, fr, cs, cr, vs, vr, hs, hr, rs, rr,
):
    s = lax.axis_index("space")
    g = lax.axis_index("group")

    def exists(way):
        ok = None
        for d, at, size in ((way[0], s, ns), (way[1], g, n)):
            if d == 0:
                continue
            here = at > 0 if d < 0 else at < size - 1
            ok = here if ok is None else jnp.logical_and(ok, here)
        return ok

    def peer(d):
        return lax.rem(g + d, n)

    def slots_of(k):
        return pl.ds(pl.multiple_of(k * CAP, CAP), CAP)

    own_copies = [
        pltpu.make_async_copy(src, dst, local.at[i])
        for i, (src, dst) in enumerate((
            (weights, w_in), (vox.at[g], gotv.at[0]),
            (feats.at[:, slots_of(g)], gotf.at[0]), (cots.at[:, slots_of(g)], gotc.at[0])))
    ]
    for c in own_copies:
        c.start()

    barrier = pltpu.get_barrier_semaphore()
    outer = [w for w in WAYS if w[0] != 0]
    for d in range(1, n):
        pl.semaphore_signal(barrier, inc=1, device_id=(s, peer(d)), device_id_type=MESH)
    for w in outer:
        @pl.when(exists(w))
        def _(w=w):
            pl.semaphore_signal(barrier, inc=1, device_id=(s + w[0], g + w[1]), device_id_type=MESH)

    for p in range(2):
        for side, d in ((0, -1), (1, 1)):
            @pl.when(jnp.logical_not(exists((d, 0))))
            def _(p=p, side=side):
                hx[p, side] = jnp.zeros((COLS // 4, 128), BF16)

            @pl.when(jnp.logical_not(exists((0, d))))
            def _(p=p, side=side):
                hy[p, side] = jnp.zeros((SIDE, LANES), BF16)

            for side2, d2 in ((0, -1), (1, 1)):
                @pl.when(jnp.logical_not(exists((d, d2))))
                def _(p=p, side=side, side2=side2):
                    hc[p, side, side2] = jnp.zeros((SIDE, 128), BF16)
    for b in range(2):
        xm[b, 0:SIDE, :] = jnp.zeros((SIDE, 3 * HALF), BF16)
        xm[b, COLS + SIDE : COLS + 2 * SIDE, :] = jnp.zeros((SIDE, 3 * HALF), BF16)
    xe[0:SIDE, :] = jnp.zeros((SIDE, 3 * 128), BF16)
    xe[COLS + SIDE : COLS + 2 * SIDE, :] = jnp.zeros((SIDE, 3 * 128), BF16)

    for dy in range(3):
        for dz in range(3):
            for i in range(HALF // C):
                for h in range(2):
                    if (i, h) not in BANDS:
                        bmf[dy, dz * HALF + i * C : dz * HALF + (i + 1) * C, h * 128 : (h + 1) * 128] = jnp.zeros(
                            (C, 128), BF16)
            bef[dy, dz * 128 : (dz + 1) * 128, :128] = jnp.zeros((128, 128), BF16)
            bef[dy, dz * 128 : (dz + 1) * 128, 128:] = jnp.zeros((128, 128), BF16)
            beb[dy, C : HALF - C, dz * 128 : (dz + 1) * 128] = jnp.zeros((HALF - 2 * C, 128), BF16)

    peers = n - 1
    for w in outer:
        peers = peers + jnp.where(exists(w), 1, 0)
    pl.semaphore_wait(barrier, peers)

    def copy_v(d):
        return pltpu.make_async_remote_copy(
            src_ref=vox.at[peer(d)], dst_ref=gotv.at[d], send_sem=vs.at[d], recv_sem=vr.at[d],
            device_id=(s, peer(d)), device_id_type=MESH)

    def copy_f(d):
        return pltpu.make_async_remote_copy(
            src_ref=feats.at[:, slots_of(peer(d))], dst_ref=gotf.at[d], send_sem=fs.at[d], recv_sem=fr.at[d],
            device_id=(s, peer(d)), device_id_type=MESH)

    def copy_c(d):
        return pltpu.make_async_remote_copy(
            src_ref=cots.at[:, slots_of(peer(d))], dst_ref=gotc.at[d], send_sem=cs.at[d], recv_sem=cr.at[d],
            device_id=(s, peer(d)), device_id_type=MESH)

    for d in range(1, n):
        copy_v(d).start()
        copy_f(d).start()
    for d in range(1, n):
        copy_c(d).start()
    for c in own_copies:
        c.wait()

    block = lax.broadcasted_iota(jnp.int32, (C, 128), 1) // C
    spread = jnp.where(
        (lax.broadcasted_iota(jnp.int32, (C, 128), 1) & (C - 1)) == lax.broadcasted_iota(jnp.int32, (C, 128), 0),
        1.0, 0.0).astype(BF16)
    tiled[...] = nn(w_in[...], spread)

    def tile(dx, dy, dz):
        a = (dx * 3 + dy) * 3 + dz
        return tiled[a * C : (a + 1) * C, :]

    for dy in range(3):
        for dz in range(3):
            w0, w1, w2 = (tile(dx, dy, dz) for dx in range(3))
            for i, h in BANDS:
                piece = 0.0
                for at, w in ((i + 1, w0), (i - 1, w2), (i, w1)):
                    if at // 4 == h:
                        piece = jnp.where(block == at % 4, w, piece)
                bmf[dy, dz * HALF + i * C : dz * HALF + (i + 1) * C, h * 128 : (h + 1) * 128] = piece.astype(BF16)
            high, low = jnp.where(block == 3, w2, 0.0).astype(BF16), jnp.where(block == 0, w0, 0.0).astype(BF16)
            bef[dy, dz * 128 : dz * 128 + C, 128:] = high
            bef[dy, dz * 128 + 3 * C : dz * 128 + 4 * C, :128] = low
            at = slice((2 - dz) * 128, (3 - dz) * 128)
            beb[2 - dy, HALF - C :, at] = low
            beb[2 - dy, 0:C, at] = high

    row = lax.broadcasted_iota(jnp.int32, (COLS, CAP), 0)

    def columns(d):
        return slice(d * CAP, (d + 1) * CAP)

    def mask(d, q, val):
        hi = jnp.broadcast_to(gotv[d] >> 8, (C, CAP))
        for x in range(SIDE):
            r0 = q * LANES + x * C
            masked[r0 : r0 + C, columns(d)] = jnp.where(hi == x, val, 0.0).astype(BF16)

    def ones(d):
        hot[:, columns(d)] = jnp.where(row == (gotv[d] & (COLS - 1)), 1.0, 0.0).astype(BF16)
        mask(d, 1, 1.0)

    ones(0)
    mask(0, 0, gotf[0].astype(F32))
    sums[...] = nt(hot[:, columns(0)], masked[0:LANES, columns(0)])
    for d in range(1, n):
        copy_v(d).wait_recv()
        ones(d)
    div[...] = 1.0 / jnp.maximum(nt(hot[...], masked[LANES : 2 * LANES, :]), 1.0)
    for d in range(1, n):
        copy_f(d).wait_recv()
        mask(d, 0, gotf[d].astype(F32))
    far_sums = nt(hot[:, CAP:], masked[0:LANES, CAP:])
    inner[0] = ((sums[...] + far_sums) * div[...]).astype(BF16)

    def shifts(val):
        z = lax.broadcasted_iota(jnp.int32, val.shape, 0) & (SIDE - 1)
        down = jnp.where(z == 0, 0.0, pltpu.roll(val, 1, 0))
        up = jnp.where(z == SIDE - 1, 0.0, pltpu.roll(val, val.shape[0] - 1, 0))
        return down.astype(BF16), val.astype(BF16), up.astype(BF16)

    lane = lax.broadcasted_iota(jnp.int32, (COLS // 4, 128), 1) // C

    def pack(val, at):
        whole = None
        for q in range(4):
            part = val[q * (COLS // 4) : (q + 1) * (COLS // 4), :]
            if q != at:
                part = pltpu.roll(part, (q - at) % 4 * C, 1)
            whole = part if whole is None else jnp.where(lane == q, part, whole)
        return whole.astype(BF16)

    def unpack(val, at):
        val = val.astype(F32)
        return jnp.concatenate(
            [val if q == at else pltpu.roll(val, (at - q) % 4 * C, 1) for q in range(4)], axis=0)

    def halo(p, k):
        dx, dy = WAYS[k]
        src_rows = pl.ds(0, SIDE) if dy < 0 else pl.ds(COLS - SIDE, SIDE)
        if dx == 0:
            src = inner.at[p, src_rows, :]
            dst = hy.at[p, 0 if dy > 0 else 1]
        elif dy == 0:
            src = packed.at[p, 0 if dx < 0 else 1]
            dst = hx.at[p, 0 if dx > 0 else 1]
        else:
            src = inner.at[p, src_rows, pl.ds(0 if dx < 0 else LANES - 128, 128)]
            dst = hc.at[p, 0 if dx > 0 else 1, 0 if dy > 0 else 1]
        return pltpu.make_async_remote_copy(
            src_ref=src, dst_ref=dst, send_sem=hs.at[p, k], recv_sem=hr.at[p, k],
            device_id=(s + dx, g + dy), device_id_type=MESH)

    def convolve(p, main, edges, dot, meanwhile):
        val = inner[p]
        for k, w in enumerate(WAYS):
            if k == 4:
                packed[p, 0] = pack(val[:, 0:128].astype(F32), 0)
                packed[p, 1] = pack(val[:, LANES - 128 :].astype(F32), 3)

            @pl.when(exists(w))
            def _(k=k):
                halo(p, k).start()
        first = lax.broadcasted_iota(jnp.int32, (1, 128), 1) < C

        def seam(v):
            v = v[:, HALF - 128 : HALF + 128].astype(F32)
            return jnp.where(first, v[:, 128:], v[:, :128])

        for b in range(2):
            for j, part in enumerate(shifts(val[:, b * HALF : (b + 1) * HALF].astype(F32))):
                xm[b, SIDE : SIDE + COLS, j * HALF : (j + 1) * HALF] = part
        for j, part in enumerate(shifts(seam(val))):
            xe[SIDE : SIDE + COLS, j * 128 : (j + 1) * 128] = part
        def row_step(dy, first_step):
            at = pl.ds(pl.multiple_of(dy * SIDE, SIDE), COLS)
            term = main(xm[:, at, :].reshape(2 * COLS, 3 * HALF), dy).reshape(2, COLS, HALF)
            inside = dot(xe[at, :], edges[dy])
            if first_step:
                acc[...] = term
            else:
                acc[...] += term
            acc[0, :, 128:] += inside[:, 128:]
            acc[1, :, :128] += inside[:, :128]

        row_step(0, True)

        @pl.loop(1, 3)
        def _(dy):
            row_step(dy, False)

        meanwhile()
        for k, w in enumerate(WAYS):
            @pl.when(exists((-w[0], -w[1])))
            def _(k=k):
                halo(p, k).wait_recv()
        for side in range(2):
            rim = hy[p, side]
            for b in range(2):
                for j, part in enumerate(shifts(rim[:, b * HALF : (b + 1) * HALF].astype(F32))):
                    xh[side, b, :, j * HALF : (j + 1) * HALF] = part
            for j, part in enumerate(shifts(seam(rim))):
                r0 = side * (COLS + 3 * SIDE)
                xf[r0 : r0 + SIDE, j * 128 : (j + 1) * 128] = part
        left, right = (
            jnp.concatenate(
                [hc[p, b, 0].astype(F32), unpack(hx[p, b], 0 if b else 3), hc[p, b, 1].astype(F32)], axis=0)
            for b in range(2))
        for j, part in enumerate(shifts(jnp.where(first, right, left))):
            xf[SIDE : COLS + 3 * SIDE, j * 128 : (j + 1) * 128] = part
        upper = dot(xf[0 : COLS + SIDE, :], edges[0])
        lower = dot(xf[3 * SIDE : COLS + 4 * SIDE, :], edges[2])
        total = upper[SIDE:] + dot(xf[2 * SIDE : COLS + 2 * SIDE, :], edges[1]) + lower[:COLS]
        acc[0, :, :128] += total[:, :128]
        acc[1, :, 128:] += total[:, 128:]
        for side, dy, r0, rim in ((0, 0, 0, upper[:SIDE]), (1, 2, COLS - SIDE, lower[COLS:])):
            at = slice(r0, r0 + SIDE)
            term = main(xh[side].reshape(2 * SIDE, 3 * HALF), dy)
            acc[:, at, :] += term.reshape(2, SIDE, HALF)
            acc[0, at, 128:] += rim[:, 128:]
            acc[1, at, :128] += rim[:, :128]

    def gate(tile_no, rows):
        at = slice(tile_no * 128, (tile_no + 1) * 128)
        half = slice(tile_no % 2 * 128, (tile_no % 2 + 1) * 128)
        o = acc[tile_no // 2, rows, half]
        sig = 1.0 / (1.0 + jnp.exp(-o))
        inner[1, rows, at] = (gy[rows, at] * sig * (1.0 + o * (1.0 - sig))).astype(BF16)

    def forward(lhs, dy):
        return nn(lhs, bmf[dy])

    def backward(lhs, dy):
        total = None
        for dz in range(3):
            flip = slice((2 - dz) * HALF, (3 - dz) * HALF)
            term = nt(lhs[:, dz * HALF : (dz + 1) * HALF], bmf[2 - dy, flip, :])
            total = term if total is None else total + term
        return total

    def first_wait():
        for d in range(n):
            if d:
                copy_c(d).wait_recv()
            mask(d, 2, gotc[d].astype(F32))
        gy[...] = nt(hot[...], masked[2 * LANES :, :])
        for tile_no in (1, 2):
            gate(tile_no, slice(SIDE, COLS - SIDE))

    convolve(0, forward, bef, nn, first_wait)
    for tile_no in (0, 3):
        gate(tile_no, slice(0, COLS))
    for tile_no in (1, 2):
        gate(tile_no, slice(0, SIDE))
        gate(tile_no, slice(COLS - SIDE, COLS))
    convolve(1, backward, beb, nt, lambda: None)

    grad = jnp.concatenate([acc[b] * div[:, b * HALF : (b + 1) * HALF] for b in range(2)], axis=1)
    grad = jnp.transpose(grad).astype(BF16)

    def copy_r(d):
        return pltpu.make_async_remote_copy(
            src_ref=back.at[d], dst_ref=out.at[:, slots_of(g)], send_sem=rs.at[d], recv_sem=rr.at[d],
            device_id=(s, peer(n - d)), device_id_type=MESH)

    def picked(d):
        hi = jnp.broadcast_to(gotv[d] >> 8, (C, CAP))
        rows = nn(grad, hot[:, slots_of(d)])
        total = jnp.zeros((C, CAP), F32)
        for x in range(SIDE):
            total = total + jnp.where(hi == x, rows[x * C : (x + 1) * C], 0.0)
        return total.astype(BF16)

    @pl.loop(1, n)
    def _(d):
        back[d] = picked(d)
        copy_r(d).start()

    out[:, slots_of(g)] = picked(0)
    for d in range(1, n):
        copy_v(d).wait_send()
        copy_f(d).wait_send()
        copy_c(d).wait_send()
    for p in range(2):
        for k, w in enumerate(WAYS):
            @pl.when(exists(w))
            def _(p=p, k=k):
                halo(p, k).wait_send()
    for d in range(1, n):
        copy_r(d).wait()


def per_device(n, ns, point_feats, point_voxel, cotangent, weights):
    slots = n * CAP
    span = COLS + 2 * SIDE
    vm = pltpu.VMEM
    dma = pltpu.SemaphoreType.DMA
    return pl.pallas_call(
        functools.partial(kernel, n, ns),
        out_shape=pltpu.VMEM((C, slots), BF16),
        in_specs=[pl.BlockSpec(memory_space=pltpu.HBM)] * 4,
        out_specs=pl.BlockSpec(memory_space=vm),
        scratch_shapes=[
            vm((n, C, CAP), BF16),
            vm((n, C, CAP), BF16),
            vm((n, 1, CAP), jnp.int32),
            vm((27 * C, C), BF16),
            vm((COLS, slots), BF16),
            vm((3 * LANES, slots), BF16),
            vm((COLS, LANES), F32),
            vm((27 * C, 128), F32),
            vm((3, 3 * HALF, HALF), BF16),
            vm((3, 3 * 128, HALF), BF16),
            vm((3, HALF, 3 * 128), BF16),
            vm((2, COLS, LANES), BF16),
            vm((2, 2, COLS // 4, 128), BF16),
            vm((2, 2, COLS // 4, 128), BF16),
            vm((2, 2, 2, SIDE, 128), BF16),
            vm((2, 2, SIDE, LANES), BF16),
            vm((2, span, 3 * HALF), BF16),
            vm((span, 3 * 128), BF16),
            vm((2, 2, SIDE, 3 * HALF), BF16),
            vm((span + 2 * SIDE, 3 * 128), BF16),
            vm((2, COLS, HALF), F32),
            vm((COLS, LANES), F32),
            vm((COLS, LANES), F32),
            vm((n, C, CAP), BF16),
            dma((4,)), dma((n,)), dma((n,)), dma((n,)), dma((n,)), dma((n,)), dma((n,)),
            dma((2, 8)), dma((2, 8)), dma((n,)), dma((n,)),
        ],
        compiler_params=pltpu.CompilerParams(
            collective_id=0, has_side_effects=True, vmem_limit_bytes=63 * 2**20
        ),
    )(point_feats.T, cotangent.T, point_voxel.reshape(n, 1, CAP), weights.reshape(27 * C, C)).T


def solution(mesh):
    n, ns = mesh.shape["group"], mesh.shape["space"]
    placed = (P(("space", "group"), None), P(("space", "group")), P(("space", "group"), None), P())
    return jax.shard_map(
        functools.partial(per_device, n, ns),
        mesh=mesh,
        in_specs=placed,
        out_specs=P(("space", "group"), None),
        check_vma=False,
    )
```

```python
import functools

import jax
import jax.numpy as jnp
from jax import lax
from jax.experimental import pallas as pl
from jax.experimental.pallas import tpu as pltpu
from jax.sharding import PartitionSpec as P

MESH = pl.DeviceIdType.MESH
F32 = jnp.float32
BF16 = jnp.bfloat16
SIDE = 16
C = 32
COLS = SIDE * SIDE
LANES = SIDE * C
HALF = LANES // 2
CAP = 256

WAYS = ((-1, -1), (-1, 1), (1, -1), (1, 1), (-1, 0), (1, 0), (0, -1), (0, 1))

OUTER_FIRST = (0, 1, 2, 3, 12, 13, 14, 15, 4, 5, 6, 7, 8, 9, 10, 11)

BANDS = tuple((i, h) for i in range(8) for h in range(2) if any(0 <= x < 8 and x // 4 == h for x in (i - 1, i, i + 1)))


def nt(a, b):
    return lax.dot_general(a, b, (((1,), (1,)), ((), ())), preferred_element_type=F32)


def nn(a, b):
    return jnp.dot(a, b, preferred_element_type=F32)


def kernel(
    n, ns, feats, cots, vox, weights, out,
    gotf, gotc, gotv, w_in, hot, masked, sums, tiled, bmf, bef, beb,
    inner, packed, hx, hc, hy, xm, xe, xh, xf, acc, gy, div, back,
    local, fs, fr, cs, cr, vs, vr, hs, hr, rs, rr,
):
    s = lax.axis_index("space")
    g = lax.axis_index("group")

    def exists(way):
        ok = None
        for d, at, size in ((way[0], s, ns), (way[1], g, n)):
            if d == 0:
                continue
            here = at > 0 if d < 0 else at < size - 1
            ok = here if ok is None else jnp.logical_and(ok, here)
        return ok

    def peer(d):
        return lax.rem(g + d, n)

    def slots_of(k):
        return pl.ds(pl.multiple_of(k * CAP, CAP), CAP)

    own_copies = [
        pltpu.make_async_copy(src, dst, local.at[i])
        for i, (src, dst) in enumerate((
            (weights, w_in), (vox.at[g], gotv.at[0]),
            (feats.at[:, slots_of(g)], gotf.at[0]), (cots.at[:, slots_of(g)], gotc.at[0])))
    ]
    for c in own_copies:
        c.start()

    barrier = pltpu.get_barrier_semaphore()
    outer = [w for w in WAYS if w[0] != 0]
    for d in range(1, n):
        pl.semaphore_signal(barrier, inc=1, device_id=(s, peer(d)), device_id_type=MESH)
    for w in outer:
        @pl.when(exists(w))
        def _(w=w):
            pl.semaphore_signal(barrier, inc=1, device_id=(s + w[0], g + w[1]), device_id_type=MESH)

    for p in range(2):
        for side, d in ((0, -1), (1, 1)):
            @pl.when(jnp.logical_not(exists((d, 0))))
            def _(p=p, side=side):
                hx[p, side] = jnp.zeros((COLS // 4, 128), BF16)

            @pl.when(jnp.logical_not(exists((0, d))))
            def _(p=p, side=side):
                hy[p, side] = jnp.zeros((SIDE, LANES), BF16)

            for side2, d2 in ((0, -1), (1, 1)):
                @pl.when(jnp.logical_not(exists((d, d2))))
                def _(p=p, side=side, side2=side2):
                    hc[p, side, side2] = jnp.zeros((SIDE, 128), BF16)
    for b in range(2):
        xm[b, 0:SIDE, :] = jnp.zeros((SIDE, 3 * HALF), BF16)
        xm[b, COLS + SIDE : COLS + 2 * SIDE, :] = jnp.zeros((SIDE, 3 * HALF), BF16)
    xe[0:SIDE, :] = jnp.zeros((SIDE, 3 * 128), BF16)
    xe[COLS + SIDE : COLS + 2 * SIDE, :] = jnp.zeros((SIDE, 3 * 128), BF16)

    for dy in range(3):
        for dz in range(3):
            for i in range(HALF // C):
                for h in range(2):
                    if (i, h) not in BANDS:
                        bmf[dy, dz * HALF + i * C : dz * HALF + (i + 1) * C, h * 128 : (h + 1) * 128] = jnp.zeros(
                            (C, 128), BF16)
            bef[dy, dz * 128 : (dz + 1) * 128, :128] = jnp.zeros((128, 128), BF16)
            bef[dy, dz * 128 : (dz + 1) * 128, 128:] = jnp.zeros((128, 128), BF16)
            beb[dy, C : HALF - C, dz * 128 : (dz + 1) * 128] = jnp.zeros((HALF - 2 * C, 128), BF16)

    peers = n - 1
    for w in outer:
        peers = peers + jnp.where(exists(w), 1, 0)
    pl.semaphore_wait(barrier, peers)

    def copy_v(d):
        return pltpu.make_async_remote_copy(
            src_ref=vox.at[peer(d)], dst_ref=gotv.at[d], send_sem=vs.at[d], recv_sem=vr.at[d],
            device_id=(s, peer(d)), device_id_type=MESH)

    def copy_f(d):
        return pltpu.make_async_remote_copy(
            src_ref=feats.at[:, slots_of(peer(d))], dst_ref=gotf.at[d], send_sem=fs.at[d], recv_sem=fr.at[d],
            device_id=(s, peer(d)), device_id_type=MESH)

    def copy_c(d):
        return pltpu.make_async_remote_copy(
            src_ref=cots.at[:, slots_of(peer(d))], dst_ref=gotc.at[d], send_sem=cs.at[d], recv_sem=cr.at[d],
            device_id=(s, peer(d)), device_id_type=MESH)

    far_first = sorted(range(1, n), key=lambda d: -min(d, n - d))
    for d in far_first:
        copy_v(d).start()
        copy_f(d).start()
    for d in far_first:
        copy_c(d).start()
    for c in own_copies:
        c.wait()

    block = lax.broadcasted_iota(jnp.int32, (C, 128), 1) // C
    spread = jnp.where(
        (lax.broadcasted_iota(jnp.int32, (C, 128), 1) & (C - 1)) == lax.broadcasted_iota(jnp.int32, (C, 128), 0),
        1.0, 0.0).astype(BF16)
    tiled[...] = nn(w_in[...], spread)

    def tile(dx, dy, dz):
        a = (dx * 3 + dy) * 3 + dz
        return tiled[a * C : (a + 1) * C, :]

    for dy in range(3):
        for dz in range(3):
            w0, w1, w2 = (tile(dx, dy, dz) for dx in range(3))
            for i, h in BANDS:
                piece = 0.0
                for at, w in ((i + 1, w0), (i - 1, w2), (i, w1)):
                    if at // 4 == h:
                        piece = jnp.where(block == at % 4, w, piece)
                bmf[dy, dz * HALF + i * C : dz * HALF + (i + 1) * C, h * 128 : (h + 1) * 128] = piece.astype(BF16)
            high, low = jnp.where(block == 3, w2, 0.0).astype(BF16), jnp.where(block == 0, w0, 0.0).astype(BF16)
            bef[dy, dz * 128 : dz * 128 + C, 128:] = high
            bef[dy, dz * 128 + 3 * C : dz * 128 + 4 * C, :128] = low
            at = slice((2 - dz) * 128, (3 - dz) * 128)
            beb[2 - dy, HALF - C :, at] = low
            beb[2 - dy, 0:C, at] = high

    row = lax.broadcasted_iota(jnp.int32, (COLS, CAP), 0)

    def columns(d):
        return slice(d * CAP, (d + 1) * CAP)

    def mask(d, q, val):
        hi = jnp.broadcast_to(gotv[d] >> 8, (C, CAP))
        for x in range(SIDE):
            r0 = q * LANES + (x if q else OUTER_FIRST.index(x)) * C
            masked[r0 : r0 + C, columns(d)] = jnp.where(hi == x, val, 0.0).astype(BF16)

    def ones(d):
        hot[:, columns(d)] = jnp.where(row == (gotv[d] & (COLS - 1)), 1.0, 0.0).astype(BF16)
        mask(d, 1, 1.0)

    ones(0)
    mask(0, 0, gotf[0].astype(F32))
    sums[...] = nt(hot[:, columns(0)], masked[0:LANES, columns(0)])
    for d in range(1, n):
        copy_v(d).wait_recv()
        ones(d)
    div[...] = 1.0 / jnp.maximum(nt(hot[...], masked[LANES : 2 * LANES, :]), 1.0)
    for d in range(1, n):
        copy_f(d).wait_recv()
        mask(d, 0, gotf[d].astype(F32))

    def shifts(val):
        z = lax.broadcasted_iota(jnp.int32, val.shape, 0) & (SIDE - 1)
        down = jnp.where(z == 0, 0.0, pltpu.roll(val, 1, 0))
        up = jnp.where(z == SIDE - 1, 0.0, pltpu.roll(val, val.shape[0] - 1, 0))
        return down.astype(BF16), val.astype(BF16), up.astype(BF16)

    lane = lax.broadcasted_iota(jnp.int32, (COLS // 4, 128), 1) // C

    def pack(val, at):
        whole = None
        for q in range(4):
            part = val[q * (COLS // 4) : (q + 1) * (COLS // 4), :]
            if q != at:
                part = pltpu.roll(part, (q - at) % 4 * C, 1)
            whole = part if whole is None else jnp.where(lane == q, part, whole)
        return whole.astype(BF16)

    def unpack(val, at):
        val = val.astype(F32)
        return jnp.concatenate(
            [val if q == at else pltpu.roll(val, (at - q) % 4 * C, 1) for q in range(4)], axis=0)

    def halo(p, k):
        dx, dy = WAYS[k]
        src_rows = pl.ds(0, SIDE) if dy < 0 else pl.ds(COLS - SIDE, SIDE)
        if dx == 0:
            src = inner.at[p, src_rows, :]
            dst = hy.at[p, 0 if dy > 0 else 1]
        elif dy == 0:
            src = packed.at[p, 0 if dx < 0 else 1]
            dst = hx.at[p, 0 if dx > 0 else 1]
        else:
            src = inner.at[p, src_rows, pl.ds(0 if dx < 0 else LANES - 128, 128)]
            dst = hc.at[p, 0 if dx > 0 else 1, 0 if dy > 0 else 1]
        return pltpu.make_async_remote_copy(
            src_ref=src, dst_ref=dst, send_sem=hs.at[p, k], recv_sem=hr.at[p, k],
            device_id=(s + dx, g + dy), device_id_type=MESH)

    def send(p, start, stop):
        for k in range(start, stop):
            @pl.when(exists(WAYS[k]))
            def _(k=k):
                halo(p, k).start()

    def send_sides(p):
        send(p, 0, 4)
        packed[p, 0] = pack(inner[p, :, 0:128].astype(F32), 0)
        packed[p, 1] = pack(inner[p, :, LANES - 128 :].astype(F32), 3)
        send(p, 4, 6)

    def convolve(p, main, edges, dot, meanwhile):
        send(p, 6, 8)
        val = inner[p]
        first = lax.broadcasted_iota(jnp.int32, (1, 128), 1) < C

        def seam(v):
            v = v[:, HALF - 128 : HALF + 128].astype(F32)
            return jnp.where(first, v[:, 128:], v[:, :128])

        for b in range(2):
            for j, part in enumerate(shifts(val[:, b * HALF : (b + 1) * HALF].astype(F32))):
                xm[b, SIDE : SIDE + COLS, j * HALF : (j + 1) * HALF] = part
        for j, part in enumerate(shifts(seam(val))):
            xe[SIDE : SIDE + COLS, j * 128 : (j + 1) * 128] = part
        def row_step(dy, first_step):
            at = pl.ds(pl.multiple_of(dy * SIDE, SIDE), COLS)
            term = main(xm[:, at, :].reshape(2 * COLS, 3 * HALF), dy).reshape(2, COLS, HALF)
            inside = dot(xe[at, :], edges[dy])
            if first_step:
                acc[...] = term
            else:
                acc[...] += term
            acc[0, :, 128:] += inside[:, 128:]
            acc[1, :, :128] += inside[:, :128]

        row_step(0, True)

        @pl.loop(1, 3)
        def _(dy):
            row_step(dy, False)

        meanwhile()
        for k, w in enumerate(WAYS):
            @pl.when(exists((-w[0], -w[1])))
            def _(k=k):
                halo(p, k).wait_recv()
        for side in range(2):
            rim = hy[p, side]
            for b in range(2):
                for j, part in enumerate(shifts(rim[:, b * HALF : (b + 1) * HALF].astype(F32))):
                    xh[side, b, :, j * HALF : (j + 1) * HALF] = part
            for j, part in enumerate(shifts(seam(rim))):
                r0 = side * (COLS + 3 * SIDE)
                xf[r0 : r0 + SIDE, j * 128 : (j + 1) * 128] = part
        left, right = (
            jnp.concatenate(
                [hc[p, b, 0].astype(F32), unpack(hx[p, b], 0 if b else 3), hc[p, b, 1].astype(F32)], axis=0)
            for b in range(2))
        for j, part in enumerate(shifts(jnp.where(first, right, left))):
            xf[SIDE : COLS + 3 * SIDE, j * 128 : (j + 1) * 128] = part
        upper = dot(xf[0 : COLS + SIDE, :], edges[0])
        lower = dot(xf[3 * SIDE : COLS + 4 * SIDE, :], edges[2])
        total = upper[SIDE:] + dot(xf[2 * SIDE : COLS + 2 * SIDE, :], edges[1]) + lower[:COLS]
        acc[0, :, :128] += total[:, :128]
        acc[1, :, 128:] += total[:, 128:]
        for side, dy, r0, rim in ((0, 0, 0, upper[:SIDE]), (1, 2, COLS - SIDE, lower[COLS:])):
            at = slice(r0, r0 + SIDE)
            term = main(xh[side].reshape(2 * SIDE, 3 * HALF), dy)
            acc[:, at, :] += term.reshape(2, SIDE, HALF)
            acc[0, at, 128:] += rim[:, 128:]
            acc[1, at, :128] += rim[:, :128]

    def gate(tile_no, rows):
        at = slice(tile_no * 128, (tile_no + 1) * 128)
        half = slice(tile_no % 2 * 128, (tile_no % 2 + 1) * 128)
        o = acc[tile_no // 2, rows, half]
        sig = 1.0 / (1.0 + jnp.exp(-o))
        inner[1, rows, at] = (gy[rows, at] * sig * (1.0 + o * (1.0 - sig))).astype(BF16)

    def forward(lhs, dy):
        return nn(lhs, bmf[dy])

    def backward(lhs, dy):
        total = None
        for dz in range(3):
            flip = slice((2 - dz) * HALF, (3 - dz) * HALF)
            term = nt(lhs[:, dz * HALF : (dz + 1) * HALF], bmf[2 - dy, flip, :])
            total = term if total is None else total + term
        return total

    def first_wait():
        for d in range(n):
            if d:
                copy_c(d).wait_recv()
            mask(d, 2, gotc[d].astype(F32))
        gy[...] = nt(hot[...], masked[2 * LANES :, :])
        for tile_no in (1, 2):
            gate(tile_no, slice(SIDE, COLS - SIDE))

    rest = sums[:, 0:HALF] + nt(hot[:, CAP:], masked[0:HALF, CAP:])
    inner[0, :, 0:128] = (rest[:, 0:128] * div[:, 0:128]).astype(BF16)
    inner[0, :, LANES - 128 :] = (rest[:, 128:] * div[:, LANES - 128 :]).astype(BF16)
    send_sides(0)
    rest = sums[:, HALF:] + nt(hot[:, CAP:], masked[HALF:LANES, CAP:])
    inner[0, :, 128 : LANES - 128] = (rest * div[:, 128 : LANES - 128]).astype(BF16)
    convolve(0, forward, bef, nn, first_wait)
    for tile_no in (0, 3):
        gate(tile_no, slice(0, COLS))
    send_sides(1)
    for tile_no in (1, 2):
        gate(tile_no, slice(0, SIDE))
        gate(tile_no, slice(COLS - SIDE, COLS))
    convolve(1, backward, beb, nt, lambda: None)

    grad = jnp.concatenate([acc[b] * div[:, b * HALF : (b + 1) * HALF] for b in range(2)], axis=1)
    grad = jnp.transpose(grad).astype(BF16)

    def copy_r(d):
        return pltpu.make_async_remote_copy(
            src_ref=back.at[d], dst_ref=out.at[:, slots_of(g)], send_sem=rs.at[d], recv_sem=rr.at[d],
            device_id=(s, peer(n - d)), device_id_type=MESH)

    def picked(d):
        hi = jnp.broadcast_to(gotv[d] >> 8, (C, CAP))
        rows = nn(grad, hot[:, slots_of(d)])
        total = jnp.zeros((C, CAP), F32)
        for x in range(SIDE):
            total = total + jnp.where(hi == x, rows[x * C : (x + 1) * C], 0.0)
        return total.astype(BF16)

    @pl.loop(1, n)
    def _(d):
        back[d] = picked(d)
        copy_r(d).start()

    out[:, slots_of(g)] = picked(0)
    for d in range(1, n):
        copy_v(d).wait_send()
        copy_f(d).wait_send()
        copy_c(d).wait_send()
    for p in range(2):
        for k, w in enumerate(WAYS):
            @pl.when(exists(w))
            def _(p=p, k=k):
                halo(p, k).wait_send()
    for d in range(1, n):
        copy_r(d).wait()


def per_device(n, ns, point_feats, point_voxel, cotangent, weights):
    slots = n * CAP
    span = COLS + 2 * SIDE
    vm = pltpu.VMEM
    dma = pltpu.SemaphoreType.DMA
    return pl.pallas_call(
        functools.partial(kernel, n, ns),
        out_shape=pltpu.VMEM((C, slots), BF16),
        in_specs=[pl.BlockSpec(memory_space=pltpu.HBM)] * 4,
        out_specs=pl.BlockSpec(memory_space=vm),
        scratch_shapes=[
            vm((n, C, CAP), BF16),
            vm((n, C, CAP), BF16),
            vm((n, 1, CAP), jnp.int32),
            vm((27 * C, C), BF16),
            vm((COLS, slots), BF16),
            vm((3 * LANES, slots), BF16),
            vm((COLS, LANES), F32),
            vm((27 * C, 128), F32),
            vm((3, 3 * HALF, HALF), BF16),
            vm((3, 3 * 128, HALF), BF16),
            vm((3, HALF, 3 * 128), BF16),
            vm((2, COLS, LANES), BF16),
            vm((2, 2, COLS // 4, 128), BF16),
            vm((2, 2, COLS // 4, 128), BF16),
            vm((2, 2, 2, SIDE, 128), BF16),
            vm((2, 2, SIDE, LANES), BF16),
            vm((2, span, 3 * HALF), BF16),
            vm((span, 3 * 128), BF16),
            vm((2, 2, SIDE, 3 * HALF), BF16),
            vm((span + 2 * SIDE, 3 * 128), BF16),
            vm((2, COLS, HALF), F32),
            vm((COLS, LANES), F32),
            vm((COLS, LANES), F32),
            vm((n, C, CAP), BF16),
            dma((4,)), dma((n,)), dma((n,)), dma((n,)), dma((n,)), dma((n,)), dma((n,)),
            dma((2, 8)), dma((2, 8)), dma((n,)), dma((n,)),
        ],
        compiler_params=pltpu.CompilerParams(
            collective_id=0, has_side_effects=True, vmem_limit_bytes=63 * 2**20
        ),
    )(point_feats.T, cotangent.T, point_voxel.reshape(n, 1, CAP), weights.reshape(27 * C, C)).T


def solution(mesh):
    n, ns = mesh.shape["group"], mesh.shape["space"]
    placed = (P(("space", "group"), None), P(("space", "group")), P(("space", "group"), None), P())
    return jax.shard_map(
        functools.partial(per_device, n, ns),
        mesh=mesh,
        in_specs=placed,
        out_specs=P(("space", "group"), None),
        check_vma=False,
    )
```

```python
import functools

import jax
import jax.numpy as jnp
from jax import lax
from jax.experimental import pallas as pl
from jax.experimental.pallas import tpu as pltpu
from jax.sharding import PartitionSpec as P

MESH = pl.DeviceIdType.MESH
F32 = jnp.float32
BF16 = jnp.bfloat16
SIDE = 16
C = 32
COLS = SIDE * SIDE
LANES = SIDE * C
HALF = LANES // 2
CAP = 256

WAYS = ((-1, -1), (-1, 1), (1, -1), (1, 1), (-1, 0), (1, 0), (0, -1), (0, 1))

BANDS = tuple((i, h) for i in range(8) for h in range(2) if any(0 <= x < 8 and x // 4 == h for x in (i - 1, i, i + 1)))


def nt(a, b):
    return lax.dot_general(a, b, (((1,), (1,)), ((), ())), preferred_element_type=F32)


def nn(a, b):
    return jnp.dot(a, b, preferred_element_type=F32)


def kernel(
    n, ns, feats, cots, vox, weights, out,
    gotf, gotc, gotv, w_in, hot, masked, sums, tiled, bmf, bef,
    inner, packed, hx, hc, hy, xm, xe, xh, xf, acc, gy, div, back,
    local, fs, fr, cs, cr, vs, vr, hs, hr, rs, rr,
):
    s = lax.axis_index("space")
    g = lax.axis_index("group")

    def exists(way):
        ok = None
        for d, at, size in ((way[0], s, ns), (way[1], g, n)):
            if d == 0:
                continue
            here = at > 0 if d < 0 else at < size - 1
            ok = here if ok is None else jnp.logical_and(ok, here)
        return ok

    def peer(d):
        return lax.rem(g + d, n)

    def slots_of(k):
        return pl.ds(pl.multiple_of(k * CAP, CAP), CAP)

    own_copies = [
        pltpu.make_async_copy(src, dst, local.at[i])
        for i, (src, dst) in enumerate((
            (weights, w_in), (vox.at[g], gotv.at[0]),
            (feats.at[:, slots_of(g)], gotf.at[0]), (cots.at[:, slots_of(g)], gotc.at[0])))
    ]
    for c in own_copies:
        c.start()

    barrier = pltpu.get_barrier_semaphore()
    outer = [w for w in WAYS if w[0] != 0]
    for d in range(1, n):
        pl.semaphore_signal(barrier, inc=1, device_id=(s, peer(d)), device_id_type=MESH)
    for w in outer:
        @pl.when(exists(w))
        def _(w=w):
            pl.semaphore_signal(barrier, inc=1, device_id=(s + w[0], g + w[1]), device_id_type=MESH)

    for p in range(2):
        for side, d in ((0, -1), (1, 1)):
            @pl.when(jnp.logical_not(exists((d, 0))))
            def _(p=p, side=side):
                hx[p, side] = jnp.zeros((COLS // 4, 128), BF16)

            @pl.when(jnp.logical_not(exists((0, d))))
            def _(p=p, side=side):
                hy[p, side] = jnp.zeros((SIDE, LANES), BF16)

            for side2, d2 in ((0, -1), (1, 1)):
                @pl.when(jnp.logical_not(exists((d, d2))))
                def _(p=p, side=side, side2=side2):
                    hc[p, side, side2] = jnp.zeros((SIDE, 128), BF16)
    for b in range(2):
        xm[b, 0:SIDE, :] = jnp.zeros((SIDE, 3 * HALF), BF16)
        xm[b, COLS + SIDE : COLS + 2 * SIDE, :] = jnp.zeros((SIDE, 3 * HALF), BF16)
    xe[0:SIDE, :] = jnp.zeros((SIDE, 3 * 128), BF16)
    xe[COLS + SIDE : COLS + 2 * SIDE, :] = jnp.zeros((SIDE, 3 * 128), BF16)

    for p in range(2):
        for dy in range(3):
            for dz in range(3):
                for i in range(HALF // C):
                    for h in range(2):
                        if (i, h) not in BANDS:
                            at = slice(dz * HALF + i * C, dz * HALF + (i + 1) * C)
                            bmf[p, dy, at, h * 128 : (h + 1) * 128] = jnp.zeros((C, 128), BF16)
            bef[p, dy] = jnp.zeros((3 * 128, HALF), BF16)

    peers = n - 1
    for w in outer:
        peers = peers + jnp.where(exists(w), 1, 0)
    pl.semaphore_wait(barrier, peers)

    def copy_v(d):
        return pltpu.make_async_remote_copy(
            src_ref=vox.at[peer(d)], dst_ref=gotv.at[d], send_sem=vs.at[d], recv_sem=vr.at[d],
            device_id=(s, peer(d)), device_id_type=MESH)

    def copy_f(d):
        return pltpu.make_async_remote_copy(
            src_ref=feats.at[:, slots_of(peer(d))], dst_ref=gotf.at[d], send_sem=fs.at[d], recv_sem=fr.at[d],
            device_id=(s, peer(d)), device_id_type=MESH)

    def copy_c(d):
        return pltpu.make_async_remote_copy(
            src_ref=cots.at[:, slots_of(peer(d))], dst_ref=gotc.at[d], send_sem=cs.at[d], recv_sem=cr.at[d],
            device_id=(s, peer(d)), device_id_type=MESH)

    for d in range(1, n):
        copy_v(d).start()
        copy_f(d).start()
    for d in range(1, n):
        copy_c(d).start()
    for c in own_copies:
        c.wait()

    block = lax.broadcasted_iota(jnp.int32, (C, 128), 1) // C
    spread = jnp.where(
        (lax.broadcasted_iota(jnp.int32, (C, 128), 1) & (C - 1)) == lax.broadcasted_iota(jnp.int32, (C, 128), 0),
        1.0, 0.0).astype(BF16)
    turned = jnp.swapaxes(w_in[...].astype(F32).reshape(27, C, C), 1, 2).reshape(27 * C, C).astype(BF16)
    tiled[0] = nn(w_in[...], spread).reshape(27, C, 128)
    tiled[1] = nn(turned, spread).reshape(27, C, 128)

    for p in range(2):
        for a in range(9):
            dy, dz = a // 3, a % 3
            w0, w1, w2 = (tiled[p, 26 - dx * 9 - a if p else dx * 9 + a] for dx in range(3))
            for i, h in BANDS:
                piece = 0.0
                for at, w in ((i + 1, w0), (i - 1, w2), (i, w1)):
                    if at // 4 == h:
                        piece = jnp.where(block == at % 4, w, piece)
                bmf[p, dy, dz * HALF + i * C : dz * HALF + (i + 1) * C, h * 128 : (h + 1) * 128] = piece.astype(BF16)
            bef[p, dy, dz * 128 : dz * 128 + C, 128:] = jnp.where(block == 3, w2, 0.0).astype(BF16)
            bef[p, dy, dz * 128 + 3 * C : dz * 128 + 4 * C, :128] = jnp.where(block == 0, w0, 0.0).astype(BF16)

    row = lax.broadcasted_iota(jnp.int32, (COLS, CAP), 0)

    def columns(d):
        return slice(d * CAP, (d + 1) * CAP)

    def mask(d, q, val):
        hi = jnp.broadcast_to(gotv[d] >> 8, (C, CAP))
        for x in range(SIDE):
            r0 = q * LANES + x * C
            masked[r0 : r0 + C, columns(d)] = jnp.where(hi == x, val, 0.0).astype(BF16)

    def ones(d):
        hot[:, columns(d)] = jnp.where(row == (gotv[d] & (COLS - 1)), 1.0, 0.0).astype(BF16)
        mask(d, 1, 1.0)

    ones(0)
    mask(0, 0, gotf[0].astype(F32))
    sums[...] = nt(hot[:, columns(0)], masked[0:LANES, columns(0)])
    for d in range(1, n):
        copy_v(d).wait_recv()
        ones(d)
    div[...] = 1.0 / jnp.maximum(nt(hot[...], masked[LANES : 2 * LANES, :]), 1.0)
    for d in range(1, n):
        copy_f(d).wait_recv()
        mask(d, 0, gotf[d].astype(F32))
    far_sums = nt(hot[:, CAP:], masked[0:LANES, CAP:])
    inner[0] = ((sums[...] + far_sums) * div[...]).astype(BF16)

    def shifts(val):
        z = lax.broadcasted_iota(jnp.int32, val.shape, 0) & (SIDE - 1)
        down = jnp.where(z == 0, 0.0, pltpu.roll(val, 1, 0))
        up = jnp.where(z == SIDE - 1, 0.0, pltpu.roll(val, val.shape[0] - 1, 0))
        return down.astype(BF16), val.astype(BF16), up.astype(BF16)

    lane = lax.broadcasted_iota(jnp.int32, (COLS // 4, 128), 1) // C

    def pack(val, at):
        whole = None
        for q in range(4):
            part = val[q * (COLS // 4) : (q + 1) * (COLS // 4), :]
            if q != at:
                part = pltpu.roll(part, (q - at) % 4 * C, 1)
            whole = part if whole is None else jnp.where(lane == q, part, whole)
        return whole.astype(BF16)

    def unpack(val, at):
        val = val.astype(F32)
        return jnp.concatenate(
            [val if q == at else pltpu.roll(val, (at - q) % 4 * C, 1) for q in range(4)], axis=0)

    def halo(p, k):
        dx, dy = WAYS[k]
        src_rows = pl.ds(0, SIDE) if dy < 0 else pl.ds(COLS - SIDE, SIDE)
        if dx == 0:
            src = inner.at[p, src_rows, :]
            dst = hy.at[p, 0 if dy > 0 else 1]
        elif dy == 0:
            src = packed.at[p, 0 if dx < 0 else 1]
            dst = hx.at[p, 0 if dx > 0 else 1]
        else:
            src = inner.at[p, src_rows, pl.ds(0 if dx < 0 else LANES - 128, 128)]
            dst = hc.at[p, 0 if dx > 0 else 1, 0 if dy > 0 else 1]
        return pltpu.make_async_remote_copy(
            src_ref=src, dst_ref=dst, send_sem=hs.at[p, k], recv_sem=hr.at[p, k],
            device_id=(s + dx, g + dy), device_id_type=MESH)

    def convolve(p, meanwhile):
        def main(lhs, dy):
            return nn(lhs, bmf[p, dy])

        def edged(lhs, dy):
            return nn(lhs, bef[p, dy])

        val = inner[p]
        for k, w in enumerate(WAYS):
            if k == 4:
                packed[p, 0] = pack(val[:, 0:128].astype(F32), 0)
                packed[p, 1] = pack(val[:, LANES - 128 :].astype(F32), 3)

            @pl.when(exists(w))
            def _(k=k):
                halo(p, k).start()
        first = lax.broadcasted_iota(jnp.int32, (1, 128), 1) < C

        def seam(v):
            v = v[:, HALF - 128 : HALF + 128].astype(F32)
            return jnp.where(first, v[:, 128:], v[:, :128])

        for b in range(2):
            for j, part in enumerate(shifts(val[:, b * HALF : (b + 1) * HALF].astype(F32))):
                xm[b, SIDE : SIDE + COLS, j * HALF : (j + 1) * HALF] = part
        for j, part in enumerate(shifts(seam(val))):
            xe[SIDE : SIDE + COLS, j * 128 : (j + 1) * 128] = part
        def row_step(dy, first_step):
            at = pl.ds(pl.multiple_of(dy * SIDE, SIDE), COLS)
            term = main(xm[:, at, :].reshape(2 * COLS, 3 * HALF), dy).reshape(2, COLS, HALF)
            inside = edged(xe[at, :], dy)
            if first_step:
                acc[...] = term
            else:
                acc[...] += term
            acc[0, :, 128:] += inside[:, 128:]
            acc[1, :, :128] += inside[:, :128]

        row_step(0, True)

        @pl.loop(1, 3)
        def _(dy):
            row_step(dy, False)

        meanwhile()
        for k, w in enumerate(WAYS):
            @pl.when(exists((-w[0], -w[1])))
            def _(k=k):
                halo(p, k).wait_recv()
        for side in range(2):
            rim = hy[p, side]
            for b in range(2):
                for j, part in enumerate(shifts(rim[:, b * HALF : (b + 1) * HALF].astype(F32))):
                    xh[side, b, :, j * HALF : (j + 1) * HALF] = part
            for j, part in enumerate(shifts(seam(rim))):
                r0 = side * (COLS + 3 * SIDE)
                xf[r0 : r0 + SIDE, j * 128 : (j + 1) * 128] = part
        left, right = (
            jnp.concatenate(
                [hc[p, b, 0].astype(F32), unpack(hx[p, b], 0 if b else 3), hc[p, b, 1].astype(F32)], axis=0)
            for b in range(2))
        for j, part in enumerate(shifts(jnp.where(first, right, left))):
            xf[SIDE : COLS + 3 * SIDE, j * 128 : (j + 1) * 128] = part
        upper = edged(xf[0 : COLS + SIDE, :], 0)
        lower = edged(xf[3 * SIDE : COLS + 4 * SIDE, :], 2)
        total = upper[SIDE:] + edged(xf[2 * SIDE : COLS + 2 * SIDE, :], 1) + lower[:COLS]
        acc[0, :, :128] += total[:, :128]
        acc[1, :, 128:] += total[:, 128:]
        for side, dy, r0, rim in ((0, 0, 0, upper[:SIDE]), (1, 2, COLS - SIDE, lower[COLS:])):
            at = slice(r0, r0 + SIDE)
            term = main(xh[side].reshape(2 * SIDE, 3 * HALF), dy)
            acc[:, at, :] += term.reshape(2, SIDE, HALF)
            acc[0, at, 128:] += rim[:, 128:]
            acc[1, at, :128] += rim[:, :128]

    def gate(tile_no, rows):
        at = slice(tile_no * 128, (tile_no + 1) * 128)
        half = slice(tile_no % 2 * 128, (tile_no % 2 + 1) * 128)
        o = acc[tile_no // 2, rows, half]
        sig = 1.0 / (1.0 + jnp.exp(-o))
        inner[1, rows, at] = (gy[rows, at] * sig * (1.0 + o * (1.0 - sig))).astype(BF16)

    def first_wait():
        for d in range(n):
            if d:
                copy_c(d).wait_recv()
            mask(d, 2, gotc[d].astype(F32))
        gy[...] = nt(hot[...], masked[2 * LANES :, :])
        for tile_no in (1, 2):
            gate(tile_no, slice(SIDE, COLS - SIDE))

    def second_input():
        for tile_no in (0, 3):
            gate(tile_no, slice(0, COLS))
        for tile_no in (1, 2):
            gate(tile_no, slice(0, SIDE))
            gate(tile_no, slice(COLS - SIDE, COLS))

    @pl.loop(0, 2)
    def _(p):
        convolve(p, lambda: pl.when(p == 0)(first_wait))
        pl.when(p == 0)(second_input)

    grad = jnp.concatenate([acc[b] * div[:, b * HALF : (b + 1) * HALF] for b in range(2)], axis=1)
    grad = jnp.transpose(grad).astype(BF16)

    def copy_r(d):
        return pltpu.make_async_remote_copy(
            src_ref=back.at[d], dst_ref=out.at[:, slots_of(g)], send_sem=rs.at[d], recv_sem=rr.at[d],
            device_id=(s, peer(n - d)), device_id_type=MESH)

    def picked(d):
        hi = jnp.broadcast_to(gotv[d] >> 8, (C, CAP))
        rows = nn(grad, hot[:, slots_of(d)])
        total = jnp.zeros((C, CAP), F32)
        for x in range(SIDE):
            total = total + jnp.where(hi == x, rows[x * C : (x + 1) * C], 0.0)
        return total.astype(BF16)

    @pl.loop(1, n)
    def _(d):
        back[d] = picked(d)
        copy_r(d).start()

    out[:, slots_of(g)] = picked(0)
    for d in range(1, n):
        copy_v(d).wait_send()
        copy_f(d).wait_send()
        copy_c(d).wait_send()
    for p in range(2):
        for k, w in enumerate(WAYS):
            @pl.when(exists(w))
            def _(p=p, k=k):
                halo(p, k).wait_send()
    for d in range(1, n):
        copy_r(d).wait()


def per_device(n, ns, point_feats, point_voxel, cotangent, weights):
    slots = n * CAP
    span = COLS + 2 * SIDE
    vm = pltpu.VMEM
    dma = pltpu.SemaphoreType.DMA
    return pl.pallas_call(
        functools.partial(kernel, n, ns),
        out_shape=pltpu.VMEM((C, slots), BF16),
        in_specs=[pl.BlockSpec(memory_space=pltpu.HBM)] * 4,
        out_specs=pl.BlockSpec(memory_space=vm),
        scratch_shapes=[
            vm((n, C, CAP), BF16),
            vm((n, C, CAP), BF16),
            vm((n, 1, CAP), jnp.int32),
            vm((27 * C, C), BF16),
            vm((COLS, slots), BF16),
            vm((3 * LANES, slots), BF16),
            vm((COLS, LANES), F32),
            vm((2, 27, C, 128), F32),
            vm((2, 3, 3 * HALF, HALF), BF16),
            vm((2, 3, 3 * 128, HALF), BF16),
            vm((2, COLS, LANES), BF16),
            vm((2, 2, COLS // 4, 128), BF16),
            vm((2, 2, COLS // 4, 128), BF16),
            vm((2, 2, 2, SIDE, 128), BF16),
            vm((2, 2, SIDE, LANES), BF16),
            vm((2, span, 3 * HALF), BF16),
            vm((span, 3 * 128), BF16),
            vm((2, 2, SIDE, 3 * HALF), BF16),
            vm((span + 2 * SIDE, 3 * 128), BF16),
            vm((2, COLS, HALF), F32),
            vm((COLS, LANES), F32),
            vm((COLS, LANES), F32),
            vm((n, C, CAP), BF16),
            dma((4,)), dma((n,)), dma((n,)), dma((n,)), dma((n,)), dma((n,)), dma((n,)),
            dma((2, 8)), dma((2, 8)), dma((n,)), dma((n,)),
        ],
        compiler_params=pltpu.CompilerParams(
            collective_id=0, has_side_effects=True, vmem_limit_bytes=63 * 2**20
        ),
    )(point_feats.T, cotangent.T, point_voxel.reshape(n, 1, CAP), weights.reshape(27 * C, C)).T


def solution(mesh):
    n, ns = mesh.shape["group"], mesh.shape["space"]
    placed = (P(("space", "group"), None), P(("space", "group")), P(("space", "group"), None), P())
    return jax.shard_map(
        functools.partial(per_device, n, ns),
        mesh=mesh,
        in_specs=placed,
        out_specs=P(("space", "group"), None),
        check_vma=False,
    )
```

```python
import functools

import jax
import jax.numpy as jnp
from jax import lax
from jax.experimental import pallas as pl
from jax.experimental.pallas import tpu as pltpu
from jax.sharding import PartitionSpec as P

MESH = pl.DeviceIdType.MESH
F32 = jnp.float32
BF16 = jnp.bfloat16
SIDE = 16
C = 32
COLS = SIDE * SIDE
LANES = SIDE * C
HALF = LANES // 2
CAP = 256

WAYS = ((-1, -1), (-1, 1), (1, -1), (1, 1), (-1, 0), (1, 0), (0, -1), (0, 1))

BANDS = tuple((i, h) for i in range(8) for h in range(2) if any(0 <= x < 8 and x // 4 == h for x in (i - 1, i, i + 1)))


def nt(a, b):
    return lax.dot_general(a, b, (((1,), (1,)), ((), ())), preferred_element_type=F32)


def nn(a, b):
    return jnp.dot(a, b, preferred_element_type=F32)


def kernel(
    n, ns, feats, cots, vox, weights, out,
    gotf, gotc, gotv, w_in, hot, masked, sums, tiled, bmf, bef, beb,
    inner, packed, hx, hc, hy, xm, xe, xh, xf, acc, gy, div, back,
    local, fs, fr, cs, cr, vs, vr, hs, hr, rs, rr,
):
    s = lax.axis_index("space")
    g = lax.axis_index("group")

    def exists(way):
        ok = None
        for d, at, size in ((way[0], s, ns), (way[1], g, n)):
            if d == 0:
                continue
            here = at > 0 if d < 0 else at < size - 1
            ok = here if ok is None else jnp.logical_and(ok, here)
        return ok

    def peer(d):
        return lax.rem(g + d, n)

    def slots_of(k):
        return pl.ds(pl.multiple_of(k * CAP, CAP), CAP)

    own_copies = [
        pltpu.make_async_copy(src, dst, local.at[i])
        for i, (src, dst) in enumerate((
            (weights, w_in), (vox.at[g], gotv.at[0]),
            (feats.at[:, slots_of(g)], gotf.at[0]), (cots.at[:, slots_of(g)], gotc.at[0])))
    ]
    for c in own_copies:
        c.start()

    barrier = pltpu.get_barrier_semaphore()
    outer = [w for w in WAYS if w[0] != 0]
    for d in range(1, n):
        pl.semaphore_signal(barrier, inc=1, device_id=(s, peer(d)), device_id_type=MESH)
    for w in outer:
        @pl.when(exists(w))
        def _(w=w):
            pl.semaphore_signal(barrier, inc=1, device_id=(s + w[0], g + w[1]), device_id_type=MESH)

    for p in range(2):
        for side, d in ((0, -1), (1, 1)):
            @pl.when(jnp.logical_not(exists((d, 0))))
            def _(p=p, side=side):
                hx[p, side] = jnp.zeros((COLS // 4, 128), BF16)

            @pl.when(jnp.logical_not(exists((0, d))))
            def _(p=p, side=side):
                hy[p, side] = jnp.zeros((SIDE, LANES), BF16)

            for side2, d2 in ((0, -1), (1, 1)):
                @pl.when(jnp.logical_not(exists((d, d2))))
                def _(p=p, side=side, side2=side2):
                    hc[p, side, side2] = jnp.zeros((SIDE, 128), BF16)
    for b in range(2):
        xm[b, 0:SIDE, :] = jnp.zeros((SIDE, 3 * HALF), BF16)
        xm[b, COLS + SIDE : COLS + 2 * SIDE, :] = jnp.zeros((SIDE, 3 * HALF), BF16)
    xe[0:SIDE, :] = jnp.zeros((SIDE, 3 * 128), BF16)
    xe[COLS + SIDE : COLS + 2 * SIDE, :] = jnp.zeros((SIDE, 3 * 128), BF16)

    for dy in range(3):
        for dz in range(3):
            for i in range(HALF // C):
                for h in range(2):
                    if (i, h) not in BANDS:
                        bmf[dy, dz * HALF + i * C : dz * HALF + (i + 1) * C, h * 128 : (h + 1) * 128] = jnp.zeros(
                            (C, 128), BF16)
            bef[dy, dz * 128 : (dz + 1) * 128, :128] = jnp.zeros((128, 128), BF16)
            bef[dy, dz * 128 : (dz + 1) * 128, 128:] = jnp.zeros((128, 128), BF16)
            beb[dy, C : HALF - C, dz * 128 : (dz + 1) * 128] = jnp.zeros((HALF - 2 * C, 128), BF16)

    peers = n - 1
    for w in outer:
        peers = peers + jnp.where(exists(w), 1, 0)
    pl.semaphore_wait(barrier, peers)

    def copy_v(d):
        return pltpu.make_async_remote_copy(
            src_ref=vox.at[peer(d)], dst_ref=gotv.at[d], send_sem=vs.at[d], recv_sem=vr.at[d],
            device_id=(s, peer(d)), device_id_type=MESH)

    def copy_f(d):
        return pltpu.make_async_remote_copy(
            src_ref=feats.at[:, slots_of(peer(d))], dst_ref=gotf.at[d], send_sem=fs.at[d], recv_sem=fr.at[d],
            device_id=(s, peer(d)), device_id_type=MESH)

    def copy_c(d):
        return pltpu.make_async_remote_copy(
            src_ref=cots.at[:, slots_of(peer(d))], dst_ref=gotc.at[d], send_sem=cs.at[d], recv_sem=cr.at[d],
            device_id=(s, peer(d)), device_id_type=MESH)

    for d in range(1, n):
        copy_v(d).start()
        copy_f(d).start()
    for d in range(1, n):
        copy_c(d).start()
    for c in own_copies:
        c.wait()

    block = lax.broadcasted_iota(jnp.int32, (C, 128), 1) // C
    spread = jnp.where(
        (lax.broadcasted_iota(jnp.int32, (C, 128), 1) & (C - 1)) == lax.broadcasted_iota(jnp.int32, (C, 128), 0),
        1.0, 0.0).astype(BF16)
    tiled[...] = nn(w_in[...], spread)

    def tile(dx, dy, dz):
        a = (dx * 3 + dy) * 3 + dz
        return tiled[a * C : (a + 1) * C, :]

    for dy in range(3):
        for dz in range(3):
            w0, w1, w2 = (tile(dx, dy, dz) for dx in range(3))
            for i, h in BANDS:
                piece = 0.0
                for at, w in ((i + 1, w0), (i - 1, w2), (i, w1)):
                    if at // 4 == h:
                        piece = jnp.where(block == at % 4, w, piece)
                bmf[dy, dz * HALF + i * C : dz * HALF + (i + 1) * C, h * 128 : (h + 1) * 128] = piece.astype(BF16)
            high, low = jnp.where(block == 3, w2, 0.0).astype(BF16), jnp.where(block == 0, w0, 0.0).astype(BF16)
            bef[dy, dz * 128 : dz * 128 + C, 128:] = high
            bef[dy, dz * 128 + 3 * C : dz * 128 + 4 * C, :128] = low
            at = slice((2 - dz) * 128, (3 - dz) * 128)
            beb[2 - dy, HALF - C :, at] = low
            beb[2 - dy, 0:C, at] = high

    row = lax.broadcasted_iota(jnp.int32, (COLS, CAP), 0)

    def columns(d):
        return slice(d * CAP, (d + 1) * CAP)

    def mask(d, q, val):
        hi = jnp.broadcast_to(gotv[d] >> 8, (C, CAP))
        for x in range(SIDE):
            r0 = q * LANES + x * C
            masked[r0 : r0 + C, columns(d)] = jnp.where(hi == x, val, 0.0).astype(BF16)

    def ones(d):
        hot[:, columns(d)] = jnp.where(row == (gotv[d] & (COLS - 1)), 1.0, 0.0).astype(BF16)
        mask(d, 1, 1.0)

    ones(0)
    mask(0, 0, gotf[0].astype(F32))
    sums[...] = nt(hot[:, columns(0)], masked[0:LANES, columns(0)])
    for d in range(1, n):
        copy_v(d).wait_recv()
        ones(d)
    div[...] = 1.0 / jnp.maximum(nt(hot[...], masked[LANES : 2 * LANES, :]), 1.0)
    for d in range(1, n):
        copy_f(d).wait_recv()
        mask(d, 0, gotf[d].astype(F32))
    far_sums = nt(hot[:, CAP:], masked[0:LANES, CAP:])
    inner[0] = ((sums[...] + far_sums) * div[...]).astype(BF16)

    def shifts(val):
        z = lax.broadcasted_iota(jnp.int32, val.shape, 0) & (SIDE - 1)
        down = jnp.where(z == 0, 0.0, pltpu.roll(val, 1, 0))
        up = jnp.where(z == SIDE - 1, 0.0, pltpu.roll(val, val.shape[0] - 1, 0))
        return down.astype(BF16), val.astype(BF16), up.astype(BF16)

    lane = lax.broadcasted_iota(jnp.int32, (COLS // 4, 128), 1) // C

    def pack(val, at):
        whole = None
        for q in range(4):
            part = val[q * (COLS // 4) : (q + 1) * (COLS // 4), :]
            if q != at:
                part = pltpu.roll(part, (q - at) % 4 * C, 1)
            whole = part if whole is None else jnp.where(lane == q, part, whole)
        return whole.astype(BF16)

    def unpack(val, at):
        val = val.astype(F32)
        return jnp.concatenate(
            [val if q == at else pltpu.roll(val, (at - q) % 4 * C, 1) for q in range(4)], axis=0)

    def halo(p, k):
        dx, dy = WAYS[k]
        src_rows = pl.ds(0, SIDE) if dy < 0 else pl.ds(COLS - SIDE, SIDE)
        if dx == 0:
            src = inner.at[p, src_rows, :]
            dst = hy.at[p, 0 if dy > 0 else 1]
        elif dy == 0:
            src = packed.at[p, 0 if dx < 0 else 1]
            dst = hx.at[p, 0 if dx > 0 else 1]
        else:
            src = inner.at[p, src_rows, pl.ds(0 if dx < 0 else LANES - 128, 128)]
            dst = hc.at[p, 0 if dx > 0 else 1, 0 if dy > 0 else 1]
        return pltpu.make_async_remote_copy(
            src_ref=src, dst_ref=dst, send_sem=hs.at[p, k], recv_sem=hr.at[p, k],
            device_id=(s + dx, g + dy), device_id_type=MESH)

    def convolve(p, main, edges, dot, meanwhile):
        val = inner[p]
        for k, w in enumerate(WAYS):
            if k == 4:
                packed[p, 0] = pack(val[:, 0:128].astype(F32), 0)
                packed[p, 1] = pack(val[:, LANES - 128 :].astype(F32), 3)

            @pl.when(exists(w))
            def _(k=k):
                halo(p, k).start()
        first = lax.broadcasted_iota(jnp.int32, (1, 128), 1) < C

        def seam(v):
            v = v[:, HALF - 128 : HALF + 128].astype(F32)
            return jnp.where(first, v[:, 128:], v[:, :128])

        for b in range(2):
            for j, part in enumerate(shifts(val[:, b * HALF : (b + 1) * HALF].astype(F32))):
                xm[b, SIDE : SIDE + COLS, j * HALF : (j + 1) * HALF] = part
        for j, part in enumerate(shifts(seam(val))):
            xe[SIDE : SIDE + COLS, j * 128 : (j + 1) * 128] = part
        def row_step(dy, first_step):
            at = pl.ds(pl.multiple_of(dy * SIDE, SIDE), COLS)
            term = main(xm[:, at, :].reshape(2 * COLS, 3 * HALF), dy).reshape(2, COLS, HALF)
            inside = dot(xe[at, :], edges[dy])
            if first_step:
                acc[...] = term
            else:
                acc[...] += term
            acc[0, :, 128:] += inside[:, 128:]
            acc[1, :, :128] += inside[:, :128]

        row_step(0, True)

        @pl.loop(1, 3)
        def _(dy):
            row_step(dy, False)

        meanwhile()
        def arrived(start, stop):
            for k in range(start, stop):
                @pl.when(exists((-WAYS[k][0], -WAYS[k][1])))
                def _(k=k):
                    halo(p, k).wait_recv()

        arrived(6, 8)
        for side in range(2):
            rim = hy[p, side]
            for b in range(2):
                for j, part in enumerate(shifts(rim[:, b * HALF : (b + 1) * HALF].astype(F32))):
                    xh[side, b, :, j * HALF : (j + 1) * HALF] = part
            for j, part in enumerate(shifts(seam(rim))):
                r0 = side * (COLS + 3 * SIDE)
                xf[r0 : r0 + SIDE, j * 128 : (j + 1) * 128] = part
        for side, dy, r0 in ((0, 0, 0), (1, 2, COLS - SIDE)):
            term = main(xh[side].reshape(2 * SIDE, 3 * HALF), dy)
            acc[:, r0 : r0 + SIDE, :] += term.reshape(2, SIDE, HALF)
        arrived(0, 6)
        left, right = (
            jnp.concatenate(
                [hc[p, b, 0].astype(F32), unpack(hx[p, b], 0 if b else 3), hc[p, b, 1].astype(F32)], axis=0)
            for b in range(2))
        for j, part in enumerate(shifts(jnp.where(first, right, left))):
            xf[SIDE : COLS + 3 * SIDE, j * 128 : (j + 1) * 128] = part
        upper = dot(xf[0 : COLS + SIDE, :], edges[0])
        lower = dot(xf[3 * SIDE : COLS + 4 * SIDE, :], edges[2])
        total = upper[SIDE:] + dot(xf[2 * SIDE : COLS + 2 * SIDE, :], edges[1]) + lower[:COLS]
        acc[0, :, :128] += total[:, :128]
        acc[1, :, 128:] += total[:, 128:]
        for r0, rim in ((0, upper[:SIDE]), (COLS - SIDE, lower[COLS:])):
            at = slice(r0, r0 + SIDE)
            acc[0, at, 128:] += rim[:, 128:]
            acc[1, at, :128] += rim[:, :128]

    def gate(tile_no, rows):
        at = slice(tile_no * 128, (tile_no + 1) * 128)
        half = slice(tile_no % 2 * 128, (tile_no % 2 + 1) * 128)
        o = acc[tile_no // 2, rows, half]
        sig = 1.0 / (1.0 + jnp.exp(-o))
        inner[1, rows, at] = (gy[rows, at] * sig * (1.0 + o * (1.0 - sig))).astype(BF16)

    def forward(lhs, dy):
        return nn(lhs, bmf[dy])

    def backward(lhs, dy):
        total = None
        for dz in range(3):
            flip = slice((2 - dz) * HALF, (3 - dz) * HALF)
            term = nt(lhs[:, dz * HALF : (dz + 1) * HALF], bmf[2 - dy, flip, :])
            total = term if total is None else total + term
        return total

    def first_wait():
        for d in range(n):
            if d:
                copy_c(d).wait_recv()
            mask(d, 2, gotc[d].astype(F32))
        gy[...] = nt(hot[...], masked[2 * LANES :, :])
        for tile_no in (1, 2):
            gate(tile_no, slice(SIDE, COLS - SIDE))

    convolve(0, forward, bef, nn, first_wait)
    for tile_no in (0, 3):
        gate(tile_no, slice(0, COLS))
    for tile_no in (1, 2):
        gate(tile_no, slice(0, SIDE))
        gate(tile_no, slice(COLS - SIDE, COLS))
    convolve(1, backward, beb, nt, lambda: None)

    grad = jnp.concatenate([acc[b] * div[:, b * HALF : (b + 1) * HALF] for b in range(2)], axis=1)
    grad = jnp.transpose(grad).astype(BF16)

    def copy_r(d):
        return pltpu.make_async_remote_copy(
            src_ref=back.at[d], dst_ref=out.at[:, slots_of(g)], send_sem=rs.at[d], recv_sem=rr.at[d],
            device_id=(s, peer(n - d)), device_id_type=MESH)

    def picked(d):
        hi = jnp.broadcast_to(gotv[d] >> 8, (C, CAP))
        rows = nn(grad, hot[:, slots_of(d)])
        total = jnp.zeros((C, CAP), F32)
        for x in range(SIDE):
            total = total + jnp.where(hi == x, rows[x * C : (x + 1) * C], 0.0)
        return total.astype(BF16)

    @pl.loop(1, n)
    def _(d):
        back[d] = picked(d)
        copy_r(d).start()

    out[:, slots_of(g)] = picked(0)
    for d in range(1, n):
        copy_v(d).wait_send()
        copy_f(d).wait_send()
        copy_c(d).wait_send()
    for p in range(2):
        for k, w in enumerate(WAYS):
            @pl.when(exists(w))
            def _(p=p, k=k):
                halo(p, k).wait_send()
    for d in range(1, n):
        copy_r(d).wait()


def per_device(n, ns, point_feats, point_voxel, cotangent, weights):
    slots = n * CAP
    span = COLS + 2 * SIDE
    vm = pltpu.VMEM
    dma = pltpu.SemaphoreType.DMA
    return pl.pallas_call(
        functools.partial(kernel, n, ns),
        out_shape=pltpu.VMEM((C, slots), BF16),
        in_specs=[pl.BlockSpec(memory_space=pltpu.HBM)] * 4,
        out_specs=pl.BlockSpec(memory_space=vm),
        scratch_shapes=[
            vm((n, C, CAP), BF16),
            vm((n, C, CAP), BF16),
            vm((n, 1, CAP), jnp.int32),
            vm((27 * C, C), BF16),
            vm((COLS, slots), BF16),
            vm((3 * LANES, slots), BF16),
            vm((COLS, LANES), F32),
            vm((27 * C, 128), F32),
            vm((3, 3 * HALF, HALF), BF16),
            vm((3, 3 * 128, HALF), BF16),
            vm((3, HALF, 3 * 128), BF16),
            vm((2, COLS, LANES), BF16),
            vm((2, 2, COLS // 4, 128), BF16),
            vm((2, 2, COLS // 4, 128), BF16),
            vm((2, 2, 2, SIDE, 128), BF16),
            vm((2, 2, SIDE, LANES), BF16),
            vm((2, span, 3 * HALF), BF16),
            vm((span, 3 * 128), BF16),
            vm((2, 2, SIDE, 3 * HALF), BF16),
            vm((span + 2 * SIDE, 3 * 128), BF16),
            vm((2, COLS, HALF), F32),
            vm((COLS, LANES), F32),
            vm((COLS, LANES), F32),
            vm((n, C, CAP), BF16),
            dma((4,)), dma((n,)), dma((n,)), dma((n,)), dma((n,)), dma((n,)), dma((n,)),
            dma((2, 8)), dma((2, 8)), dma((n,)), dma((n,)),
        ],
        compiler_params=pltpu.CompilerParams(
            collective_id=0, has_side_effects=True, vmem_limit_bytes=63 * 2**20
        ),
    )(point_feats.T, cotangent.T, point_voxel.reshape(n, 1, CAP), weights.reshape(27 * C, C)).T


def solution(mesh):
    n, ns = mesh.shape["group"], mesh.shape["space"]
    placed = (P(("space", "group"), None), P(("space", "group")), P(("space", "group"), None), P())
    return jax.shard_map(
        functools.partial(per_device, n, ns),
        mesh=mesh,
        in_specs=placed,
        out_specs=P(("space", "group"), None),
        check_vma=False,
    )
```
